512 devices in a mesh: wide: 64 (over z, x_hi, core), narrow: 8 (over y, x_lo).
Axes of the slice: x: 4 (x_hi: 2, x_lo: 2; x = x_hi * 2 + x_lo), y: 4, z: 16, core: 2. Of those that a mesh axis runs over, the one named last changes fastest.
Arguments:
- heat_power: float32 [8192, 8192], P('wide', 'narrow'), may hold values from 0 to 40, as said below
- level_taps: float32 [3, 17], replicated, may hold values from 0.02 to 0.1
- top_rows: float32 [1024, 1024], P('wide'), may hold values from 0 to 0.75
- top_cols: float32 [1024, 1024], P('narrow'), may hold values from 0 to 0.75
Outputs:
- temperature: float32 [8192, 8192], P('wide', 'narrow')
The draws below stay inside these ranges and needn't reach their ends.
Inputs may be any that keep to these rules, and one draw needn't show every extreme that they name: `heat_power`: heater powers, not negative.
All inputs are finite; a program needn't handle non-finite values.
Results may differ from the reference program's by a relative error of at most 0.000053.
Values sent between devices are 32-bit elements; how exact they have to be, the bound alone decides.
A program may use at most 64 MiB of HBM per device.

```python
import jax
import jax.numpy as jnp
from jax import lax

RADIUS = 8
GRID_ROWS = 8192
GRID_COLS = 8192
TOP_ROWS = 1024
TOP_COLS = 1024


def kernel_piece(key, order, reach):
    rows_at = jnp.arange(order)[:, None]
    cols_at = jnp.arange(order)[None, :]
    spacing = jnp.abs(rows_at - cols_at).astype(jnp.float32)
    smooth_part = 1.0 / jnp.sqrt(1.0 + (spacing / reach) ** 2)
    uniform_part = jax.random.uniform(key, (order, order), jnp.float32)
    rough_part = 0.5 + uniform_part
    off_part = 0.45 / order * smooth_part * rough_part
    return jnp.where(rows_at == cols_at, 0.75, off_part).astype(jnp.float32)


def draw_top_rows(key, part):
    key = jax.random.fold_in(key, 11)
    return kernel_piece(key, TOP_ROWS, TOP_ROWS / 4.0)


def draw_top_cols(key, part):
    key = jax.random.fold_in(key, 23)
    return kernel_piece(key, TOP_COLS, TOP_COLS / 4.0)


def draw_heat_power(key, part):
    key = jax.random.fold_in(key, 5)
    region_key, cell_key = jax.random.split(key)
    region_rows = (GRID_ROWS + 63) // 64
    region_cols = (GRID_COLS + 63) // 64
    region_draw = jax.random.uniform(region_key, (region_rows, region_cols), jnp.float32)
    cell_draw = jax.random.uniform(cell_key, (GRID_ROWS, GRID_COLS), jnp.float32)
    region_level = jnp.exp(jnp.log(0.1) + region_draw * (jnp.log(10.0) - jnp.log(0.1)))
    cell_level = 0.25 + 1.5 * cell_draw
    spread_level = jnp.repeat(jnp.repeat(region_level, 64, 0), 64, 1)[:GRID_ROWS, :GRID_COLS]
    return (spread_level * cell_level).astype(jnp.float32)


def setup_inputs(seed: int = 0) -> dict:
    splits = jax.random.split(jax.random.key(seed), 5)
    return {
        "heat_power": draw_heat_power(jax.random.fold_in(splits[4], 71), 0),
        "level_taps": jnp.clip(jax.random.uniform(splits[1], (3, 2 * RADIUS + 1), jnp.float32, 0.02, 0.1), 0.02, 0.1),
        "top_rows": draw_top_rows(jax.random.fold_in(splits[4], 71), 0),
        "top_cols": draw_top_cols(jax.random.fold_in(splits[4], 71), 0),
    }


def pad_along(field, margin, along):
    widths = [(0, 0), (0, 0)]
    widths[along] = (margin, margin)
    return jnp.pad(field, widths)


def stencil_along(padded, along, weights):
    count = weights.shape[0]
    length = padded.shape[along] - count + 1
    result = weights[0] * lax.slice_in_dim(padded, 0, length, axis=along)
    for offset in range(1, count):
        result = result + weights[offset] * lax.slice_in_dim(padded, offset, offset + length, axis=along)
    return result


def restrict_along(padded, along):
    length = padded.shape[along] - 2
    picks = [lax.slice_in_dim(padded, offset, offset + length - 1, stride=2, axis=along) for offset in range(4)]
    return (picks[0] + picks[3]) * 0.125 + (picks[1] + picks[2]) * 0.375


def prolong_along(padded, along):
    length = padded.shape[along] - 2
    left_part = lax.slice_in_dim(padded, 0, length, axis=along)
    centre = lax.slice_in_dim(padded, 1, length + 1, axis=along)
    right_part = lax.slice_in_dim(padded, 2, length + 2, axis=along)
    even_cells = 0.75 * centre + 0.25 * left_part
    odd_cells = 0.75 * centre + 0.25 * right_part
    joined = jnp.stack([even_cells, odd_cells], along + 1)
    target = list(centre.shape)
    target[along] = 2 * length
    return joined.reshape(target)


def both_ways(field, margin, along_fn):
    rows_done = along_fn(pad_along(field, margin, 0), 0)
    return along_fn(pad_along(rows_done, margin, 1), 1)


def reference(heat_power, level_taps, top_rows, top_cols):
    margin = (level_taps.shape[1] - 1) // 2
    fields = [heat_power]
    for tier_index in range(3):
        fields.append(both_ways(fields[-1], 1, restrict_along))
    coarse = jnp.dot(jnp.dot(top_rows, fields[3], precision=lax.Precision.HIGHEST), top_cols.T, precision=lax.Precision.HIGHEST)
    for tier_index in (2, 1, 0):
        weights = level_taps[tier_index]

        def apply_taps(padded, along, weights=weights):
            return stencil_along(padded, along, weights)

        coarse = both_ways(fields[tier_index], margin, apply_taps) + both_ways(coarse, 1, prolong_along)
    return coarse
```

```python
import functools

import jax
import jax.numpy as jnp
import ml_dtypes
import numpy as np
from jax import lax
from jax.experimental import pallas as pl
from jax.experimental.pallas import tpu as pltpu
from jax.sharding import PartitionSpec as P

F32 = jnp.float32
BF16 = jnp.bfloat16
MESH = pl.DeviceIdType.MESH
TAPS = 17
NZ, NQ, NN = 16, 4, 8
NW = NZ * NQ
ROWS, COLS = 128, 1024
HALO = 40
EXT = ROWS + 2 * HALO
SIDE = 128
WIDE = COLS + 2 * SIDE
TILE = 256
WIN = TILE + 2 * SIDE


def restriction(out_n, out_off, in_n, in_off, first, out_end, in_end):
    out_at = np.arange(out_n)[:, None] + out_off
    in_at = np.arange(in_n)[None, :] + in_off
    d = in_at - 2 * out_at
    m = np.where((d == 0) | (d == 1), 0.375, 0.0) + np.where((d == -1) | (d == 2), 0.125, 0.0)
    if first:
        m = np.where((out_at >= 0) & (in_at >= 0), m, 0.0)
    if out_end is not None:
        m = np.where((out_at < out_end) & (in_at < in_end), m, 0.0)
    return m


def prolongation(out_n, out_off, in_n, in_off, first, in_end):
    out_at = np.arange(out_n)[:, None] + out_off
    in_at = np.arange(in_n)[None, :] + in_off
    d = out_at - 2 * in_at
    m = np.where((d == 0) | (d == 1), 0.75, 0.0) + np.where((d == -1) | (d == 2), 0.25, 0.0)
    if first:
        m = np.where(in_at >= 0, m, 0.0)
    if in_end is not None:
        m = np.where(in_at < in_end, m, 0.0)
    return m


def level_maps(block, off, size, variant):
    first, last = variant == 0, variant == 2
    end = [block >> t if last else None for t in range(4)]
    r1 = restriction(size // 2, -off // 2, size, -off, first, end[1], end[0])
    r2 = restriction(size // 4, -off // 4, size // 2, -off // 2, first, end[2], end[1])
    r3 = restriction(block // 8, 0, size // 4, -off // 4, first, end[3], end[2])
    p1 = prolongation(block, 0, size // 2, -off // 2, first, end[1])
    p2 = prolongation(size // 2, -off // 2, size // 4, -off // 4, first, end[2])
    return r1, r2, r3, p1, p2


def top_prolong(block, in_n, in_off, variant):
    first, last = variant == 0, variant == 2
    end = [block >> t if last else None for t in range(4)]
    p3 = prolongation(block // 4 + 4, -2, in_n, in_off, first, end[3])
    p2 = prolongation(block // 2 + 4, -2, block // 4 + 4, -2, first, end[2])
    p1 = prolongation(block, 0, block // 2 + 4, -2, first, end[1])
    return p1 @ p2 @ p3


def padded(m, rows, cols):
    out = np.zeros((rows, cols))
    out[: m.shape[0], : m.shape[1]] = m
    return out


ROW_AT = dict(r3=(0, 16), r1=(16, 128), r21=(144, 64), p1=(208, 128), p12=(336, 128), top=(464, 128))
COL_AT = dict(r1=(0, 512), r21=(512, 512), p1=(1024, 256), p12=(1280, 128))


def constants():
    row_maps, col_maps, col_top, col_res = [], [], [], []
    for v in range(3):
        r1, r2, r3, p1, p2 = level_maps(ROWS, HALO, EXT, v)
        row_maps.append(
            np.concatenate(
                [
                    padded((r3 @ r2 @ r1)[:, HALO - 8 : HALO + ROWS + 8], 16, 256),
                    padded(r1, 128, 256),
                    padded(r2 @ r1, 64, 256),
                    padded(p1, 128, 256),
                    padded(p1 @ p2, 128, 256),
                    padded(top_prolong(ROWS, 24, -1, v), 128, 256),
                ]
            )
        )
        r1, r2, r3, p1, p2 = level_maps(TILE, SIDE, WIN, v)
        col_maps.append(
            np.concatenate(
                [r1.T, padded((r2 @ r1).T, 512, 256), p1.T, (p1 @ p2).T]
            )
        )
        r1, r2, r3, p1, p2 = level_maps(COLS, SIDE, WIDE, v)
        col_res.append((r3 @ r2 @ r1).T)
        col_top.append(top_prolong(COLS, 144, -8, v).T)
    as_bf16 = lambda ms: np.stack(ms).astype(ml_dtypes.bfloat16)
    return as_bf16(row_maps), as_bf16(col_maps), as_bf16(col_res), as_bf16(col_top)


def split(x):
    hi = x.astype(BF16)
    return hi, (x - hi.astype(F32)).astype(BF16)


def mm(a, b):
    return jnp.dot(a, b, preferred_element_type=F32)


def mm3(ah, al, bh, bl):
    return mm(ah, bh) + (mm(al, bh) + mm(ah, bl))


def mm_nt(a, b):
    return lax.dot_general(a, b, (((1,), (1,)), ((), ())), preferred_element_type=F32)


def band(shape, in_dim, shift, taps, level):
    d = (
        lax.broadcasted_iota(jnp.int32, shape, in_dim)
        - lax.broadcasted_iota(jnp.int32, shape, 1 - in_dim)
        + shift
    )
    out = jnp.zeros(shape, F32)
    for k in range(TAPS):
        out = jnp.where(d == k, taps[level, k], out)
    return out


def between(shape, dim, low, high):
    at = lax.broadcasted_iota(jnp.int32, shape, dim)
    return (at >= low) & (at < high)


def kernel(
    heat, taps, top_rows, top_cols, row_maps, col_maps, col_res, col_top, out,
    q, aa, at, ab, bx, rmap, cmap, cres, ctop,
    mr_h, mr_l, y_h, y_l, n_h, n_l, a_h, a_l,
    g, ps, pb, xb,
    load_sem, near_s, near_r, far_s, far_r, aa_s, aa_r, ah_s, ah_r, bx_s, bx_r,
    z1_s, z1_r, z2_s, z2_r, pb_s, pb_r, xb_s, xb_r,
):
    w, n = lax.axis_index("wide"), lax.axis_index("narrow")
    z, qi = w // NQ, w % NQ

    def dev(dw, dn):
        return ((w + dw + NW) % NW, (n + dn + NN) % NN)

    def in_z(dz):
        return (((z + dz + NZ) % NZ) * NQ + qi, n)

    def in_plane(k):
        return (z * NQ + (qi + k + NQ) % NQ, n)

    row_v = jnp.where(w == 0, 0, jnp.where(w == NW - 1, 2, 1))
    col_v = jnp.where(n == 0, 0, jnp.where(n == NN - 1, 2, 1))

    loads = [
        pltpu.make_async_copy(heat, q.at[HALO : HALO + ROWS, SIDE : SIDE + COLS], load_sem.at[0]),
        pltpu.make_async_copy(top_rows, aa.at[qi], load_sem.at[1]),
        pltpu.make_async_copy(top_cols, bx.at[8:136], load_sem.at[2]),
        pltpu.make_async_copy(row_maps.at[row_v], rmap, load_sem.at[3]),
        pltpu.make_async_copy(col_res.at[col_v], cres, load_sem.at[4]),
        pltpu.make_async_copy(col_maps.at[1], cmap.at[0], load_sem.at[5]),
        pltpu.make_async_copy(col_maps.at[col_v], cmap.at[1], load_sem.at[6]),
        pltpu.make_async_copy(col_top.at[col_v], ctop, load_sem.at[7]),
    ]
    for c in loads:
        c.start()

    barrier = pltpu.get_barrier_semaphore()
    turn = 2 - 4 * (z % 2)
    around = [(dw, dn) for dw in (-1, 0, 1) for dn in (-1, 0, 1) if (dw, dn) != (0, 0)]
    greet = [dev(dw, dn) for dw, dn in around]
    greet += [in_plane(-k) for k in (1, 2, 3)]
    greet += [dev(0, k) for k in (2, 3, 4, 5, 6)]
    greet += [in_z(-dz) for dz in (1, -1, 4, -4, 8)] + [in_z(-turn)]
    count = len(greet)
    greet += [(((z + NZ - 1) % NZ) * NQ + NQ - 1, n), (((z + 1) % NZ) * NQ, n)]
    for target in greet:
        pl.semaphore_signal(barrier, inc=1, device_id=target, device_id_type=MESH)
    pl.semaphore_wait(barrier, jnp.where((qi == 0) | (qi == NQ - 1), count + NQ, count))

    def send(src, dst, send_sem, recv_sem, target):
        c = pltpu.make_async_remote_copy(
            src_ref=src, dst_ref=dst, send_sem=send_sem, recv_sem=recv_sem,
            device_id=target, device_id_type=MESH,
        )
        c.start()
        return c

    near_rows = {1: (ROWS + HALO - 8, HALO - 8, 8), -1: (HALO, HALO + ROWS, 8)}
    far_rows = {1: (ROWS + HALO - 40, 0, 32), -1: (HALO + 8, HALO + ROWS + 8, 32)}
    same_rows = (HALO, HALO, ROWS)
    cols_of = {1: (COLS, 0, SIDE), -1: (SIDE, SIDE + COLS, SIDE), 0: (SIDE, SIDE, COLS)}

    def halo(rows, dw, dn, i, s_sem, r_sem):
        sr, tr, nr = rows
        sc, tc, nc = cols_of[dn]
        return send(
            q.at[sr : sr + nr, sc : sc + nc], q.at[tr : tr + nr, tc : tc + nc],
            s_sem.at[i], r_sem.at[i], dev(dw, dn),
        )

    loads[0].wait()
    near = [
        halo(near_rows[dw] if dw else same_rows, dw, dn, i, near_s, near_r)
        for i, (dw, dn) in enumerate(around)
    ]
    loads[1].wait()
    plane = [
        send(aa.at[qi], aa.at[qi], aa_s.at[k - 1], aa_r.at[k - 1], in_plane(k)) for k in (1, 2, 3)
    ]

    def rim_copy(src, dst, side, p, dz):
        return pltpu.make_async_remote_copy(
            src_ref=src, dst_ref=dst, send_sem=ah_s.at[p], recv_sem=ah_r.at[side],
            device_id=(((z + dz + NZ) % NZ) * NQ + p, n), device_id_type=MESH,
        )

    @pl.when(qi == NQ - 1)
    def _():
        for p in range(NQ):
            rim_copy(aa.at[NQ - 1, 8:16], at, 0, p, 1).start()

    @pl.when(qi == 0)
    def _():
        for p in range(NQ):
            rim_copy(aa.at[0, 0:8], ab, 1, p, -1).start()

    loads[2].wait()
    sides = [
        send(bx.at[128:136], bx.at[0:8], bx_s.at[0], bx_r.at[0], dev(0, 1)),
        send(bx.at[8:16], bx.at[136:144], bx_s.at[1], bx_r.at[1], dev(0, -1)),
    ]
    updown = [(dw, dn) for dw, dn in around if dw]
    far = [halo(far_rows[dw], dw, dn, i, far_s, far_r) for i, (dw, dn) in enumerate(updown)]

    loads[3].wait()

    def rm(name, cols):
        start, rows = ROW_AT[name]
        return rmap[start : start + rows, 0:cols]

    low, high = jnp.where(w == 0, HALO, 0), jnp.where(w == NW - 1, HALO + ROWS, EXT)
    t0 = jnp.where(
        between((ROWS, EXT), 1, low, high), band((ROWS, EXT), 1, 8 - HALO, taps, 0), 0.0
    )

    def row_level(level, size, res, pro):
        th, tl = split(band((size, size), 1, 8, taps, level))
        tr_h, tr_l = split(mm(th, res) + mm(tl, res))
        return mm(pro, tr_h) + mm(pro, tr_l)

    for i, m in enumerate(
        (t0, row_level(1, 128, rm("r1", EXT), rm("p1", 128)), row_level(2, 64, rm("r21", EXT), rm("p12", 64)))
    ):
        hi, lo = split(m)
        mr_h[i * ROWS : (i + 1) * ROWS, :] = hi
        mr_l[i * ROWS : (i + 1) * ROWS, :] = lo

    loads[4].wait()
    for c in near:
        c.wait_recv()
    q_hi, q_lo = split(q[HALO - 8 : HALO + ROWS + 8, :])
    r3 = rm("r3", ROWS + 16)
    by_rows_h, by_rows_l = split(mm(r3, q_hi) + mm(r3, q_lo))
    c3 = cres[...]
    slot, lane = z % 4, z // 4
    g[slot, lane] = mm(by_rows_h, c3) + mm(by_rows_l, c3)

    first_stage = [
        send(g.at[slot, lane], g.at[slot, lane], z1_s.at[i], z1_r.at[i], in_z(dz))
        for i, dz in enumerate((4, -4, 8))
    ]

    def col_maps_of(i, low, high):
        def cm(name, cols):
            start, rows = COL_AT[name]
            return cmap[i, start : start + rows, 0:cols]

        m = jnp.where(
            between((WIN, TILE), 0, low, high), band((WIN, TILE), 0, 8 - SIDE, taps, 0), 0.0
        )
        n_h[i, 0], n_l[i, 0] = split(m)
        for level, size, res, pro in (
            (1, 256, cm("r1", 256), cm("p1", 256)),
            (2, 128, cm("r21", 128), cm("p12", 256)),
        ):
            th, tl = split(band((size, size), 0, 8, taps, level))
            tp_h, tp_l = split(mm(th, pro) + mm(tl, pro))
            n_h[i, level], n_l[i, level] = split(mm(res, tp_h) + mm(res, tp_l))

    loads[5].wait()
    col_maps_of(0, 0, WIN)

    for c in first_stage:
        c.wait_recv()
    second_stage = [
        send(g.at[slot], g.at[slot], z2_s.at[i], z2_r.at[i], in_z(dz))
        for i, dz in enumerate((1, -1, turn))
    ]

    for c in plane:
        c.wait_recv()
    for side, dst in ((0, at), (1, ab)):
        rim_copy(dst, dst, side, 0, 1).wait_recv()
    m_at = lax.broadcasted_iota(jnp.int32, (COLS, 256), 1)
    wanted = 64 * (4 * ((m_at // 16) % 4) + m_at // 64) + 16 * qi + m_at % 16
    pick = jnp.where(lax.broadcasted_iota(jnp.int32, (COLS, 256), 0) == wanted, 1.0, 0.0).astype(BF16)
    top_h, top_l = split(
        jnp.concatenate([at[...], aa[0], aa[1], aa[2], aa[3], ab[...]], axis=0)
    )
    a_h[...] = mm(top_h, pick).astype(BF16)
    a_l[...] = mm(top_l, pick).astype(BF16)

    loads[6].wait()
    col_maps_of(
        1,
        jnp.where(n == 0, SIDE, 0),
        jnp.where(n == NN - 1, SIDE + TILE, WIN),
    )

    for c in second_stage:
        c.wait_recv()
    gathered = jnp.concatenate([g[r, s] for r in range(4) for s in range(4)], axis=0)
    g_h, g_l = split(gathered)
    ps[...] = mm3(a_h[...], a_l[...], g_h, g_l)
    partial_sums = []
    for k in (1, 2, 3):
        start = pl.multiple_of(16 * ((qi + k) % NQ), 16)
        partial_sums.append(
            send(ps.at[pl.ds(start, 32)], pb.at[k - 1], pb_s.at[k - 1], pb_r.at[k - 1], in_plane(k))
        )

    for c in far:
        c.wait_recv()
    for j in range(WIDE // 256):
        at_j = slice(256 * j, 256 * (j + 1))
        q_hi, q_lo = split(q[:, at_j])
        hi, lo = split(mm3(mr_h[...], mr_l[...], q_hi, q_lo))
        y_h[:, at_j] = hi
        y_l[:, at_j] = lo

    for c in partial_sums:
        c.wait_recv()
    own = pl.multiple_of(16 * qi, 16)
    total = (ps[pl.ds(own, 32), :] + pb[0]) + (pb[1] + pb[2])
    xb[n] = total[7:31, :]
    lines = [
        send(xb.at[n], xb.at[n], xb_s.at[k - 1], xb_r.at[k - 1], dev(0, k)) for k in range(1, NN)
    ]

    last = COLS // TILE - 1
    for j in range(last + 1):
        which = 0
        if j == 0:
            which = jnp.where(n == 0, 1, 0)
        if j == last:
            which = jnp.where(n == NN - 1, 1, 0)
        acc = None
        for t in range(3):
            rows = slice(t * ROWS, (t + 1) * ROWS)
            cols = slice(TILE * j, TILE * j + WIN)
            term = mm3(y_h[rows, cols], y_l[rows, cols], n_h[which, t], n_l[which, t])
            acc = term if acc is None else acc + term
        out[:, TILE * j : TILE * (j + 1)] = acc

    for c in sides:
        c.wait_recv()
    b_h, b_l = split(bx[...])
    loads[7].wait()

    for c in lines:
        c.wait_recv()
    x_h, x_l = split(jnp.concatenate([xb[i] for i in range(NN)], axis=1))
    e_h, e_l = split(mm_nt(x_h, b_h) + (mm_nt(x_l, b_h) + mm_nt(x_h, b_l)))
    up = ctop[...]
    f_h, f_l = split(mm(e_h, up) + mm(e_l, up))
    ur = rm("top", 24)
    out[...] += mm(ur, f_h) + mm(ur, f_l)

    for c in near + plane + sides + far + first_stage + second_stage + partial_sums + lines:
        c.wait_send()

    @pl.when(qi == NQ - 1)
    def _():
        for p in range(NQ):
            rim_copy(aa.at[NQ - 1, 8:16], at, 0, p, 1).wait_send()

    @pl.when(qi == 0)
    def _():
        for p in range(NQ):
            rim_copy(aa.at[0, 0:8], ab, 1, p, -1).wait_send()


def shards(maps, heat_power, level_taps, top_rows, top_cols):
    anywhere = pl.BlockSpec(memory_space=pl.ANY)
    dma = lambda k: pltpu.SemaphoreType.DMA((k,))
    sems = [8, 8, 8, 6, 6, 3, 3, 4, 2, 2, 2, 3, 3, 3, 3, 3, 3, 7, 7]
    return pl.pallas_call(
        kernel,
        out_shape=jax.ShapeDtypeStruct((ROWS, COLS), F32),
        in_specs=[anywhere, pl.BlockSpec(memory_space=pltpu.SMEM)] + [anywhere] * 6,
        out_specs=pl.BlockSpec(memory_space=pltpu.VMEM),
        scratch_shapes=[
            pltpu.VMEM((EXT, WIDE), F32),
            pltpu.VMEM((NQ, 16, COLS), F32),
            pltpu.VMEM((8, COLS), F32),
            pltpu.VMEM((8, COLS), F32),
            pltpu.VMEM((144, COLS), F32),
            pltpu.VMEM(maps[0].shape[1:], BF16),
            pltpu.VMEM((2,) + maps[1].shape[1:], BF16),
            pltpu.VMEM(maps[2].shape[1:], BF16),
            pltpu.VMEM(maps[3].shape[1:], BF16),
            pltpu.VMEM((3 * ROWS, EXT), BF16),
            pltpu.VMEM((3 * ROWS, EXT), BF16),
            pltpu.VMEM((3 * ROWS, WIDE), BF16),
            pltpu.VMEM((3 * ROWS, WIDE), BF16),
            pltpu.VMEM((2, 3, WIN, TILE), BF16),
            pltpu.VMEM((2, 3, WIN, TILE), BF16),
            pltpu.VMEM((80, 256), BF16),
            pltpu.VMEM((80, 256), BF16),
            pltpu.VMEM((4, 4, 16, 128), F32),
            pltpu.VMEM((80, 128), F32),
            pltpu.VMEM((3, 32, 128), F32),
            pltpu.VMEM((NN, 24, 128), F32),
        ]
        + [dma(k) for k in sems],
        compiler_params=pltpu.CompilerParams(
            collective_id=0, has_side_effects=True, vmem_limit_bytes=48 * 1024 * 1024
        ),
    )(heat_power, level_taps, top_rows, top_cols, *maps)


def solution(mesh):
    maps = constants()
    return jax.shard_map(
        functools.partial(shards, maps),
        mesh=mesh,
        in_specs=(P("wide", "narrow"), P(), P("wide", None), P("narrow", None)),
        out_specs=P("wide", "narrow"),
        check_vma=False,
    )
```

```python
import functools

import jax
import jax.numpy as jnp
import ml_dtypes
import numpy as np
from jax import lax
from jax.experimental import pallas as pl
from jax.experimental.pallas import tpu as pltpu
from jax.sharding import PartitionSpec as P

F32 = jnp.float32
BF16 = jnp.bfloat16
MESH = pl.DeviceIdType.MESH
TAPS = 17
NZ, NQ, NN, NY = 16, 4, 8, 4
NW = NZ * NQ
ROWS, COLS = 128, 1024
HALO = 40
EXT = ROWS + 2 * HALO
SIDE = 128
WIDE = COLS + 2 * SIDE
TILE = 128
MARGIN = 64
WIN = TILE + 2 * MARGIN
SPAN = COLS + 2 * MARGIN
TILES = COLS // TILE


def restriction(out_n, out_off, in_n, in_off, first, out_end, in_end):
    out_at = np.arange(out_n)[:, None] + out_off
    in_at = np.arange(in_n)[None, :] + in_off
    d = in_at - 2 * out_at
    m = np.where((d == 0) | (d == 1), 0.375, 0.0) + np.where((d == -1) | (d == 2), 0.125, 0.0)
    if first:
        m = np.where((out_at >= 0) & (in_at >= 0), m, 0.0)
    if out_end is not None:
        m = np.where((out_at < out_end) & (in_at < in_end), m, 0.0)
    return m


def prolongation(out_n, out_off, in_n, in_off, first, in_end):
    out_at = np.arange(out_n)[:, None] + out_off
    in_at = np.arange(in_n)[None, :] + in_off
    d = out_at - 2 * in_at
    m = np.where((d == 0) | (d == 1), 0.75, 0.0) + np.where((d == -1) | (d == 2), 0.25, 0.0)
    if first:
        m = np.where(in_at >= 0, m, 0.0)
    if in_end is not None:
        m = np.where(in_at < in_end, m, 0.0)
    return m


def level_maps(block, off, size, variant):
    first, last = variant == 0, variant == 2
    end = [block >> t if last else None for t in range(4)]
    r1 = restriction(size // 2, -off // 2, size, -off, first, end[1], end[0])
    r2 = restriction(size // 4, -off // 4, size // 2, -off // 2, first, end[2], end[1])
    p1 = prolongation(block, 0, size // 2, -off // 2, first, end[1])
    p2 = prolongation(size // 2, -off // 2, size // 4, -off // 4, first, end[2])
    return r1, r2, p1, p2


def top_prolong(block, in_n, in_off, variant):
    first, last = variant == 0, variant == 2
    end = [block >> t if last else None for t in range(4)]
    p3 = prolongation(block // 4 + 4, -2, in_n, in_off, first, end[3])
    p2 = prolongation(block // 2 + 4, -2, block // 4 + 4, -2, first, end[2])
    p1 = prolongation(block, 0, block // 2 + 4, -2, first, end[1])
    return p1 @ p2 @ p3


def own_to_top(block, variant):
    first, last = variant == 0, variant == 2
    end = [block >> t if last else None for t in range(4)]
    r1 = restriction(block // 2 + 16, -8, block, 0, first, end[1], end[0])
    r2 = restriction(block // 4 + 16, -8, block // 2 + 16, -8, first, end[2], end[1])
    r3 = restriction(block // 8 + 16, -8, block // 4 + 16, -8, first, end[3], end[2])
    return r3 @ r2 @ r1


def padded(m, rows, cols):
    out = np.zeros((rows, cols))
    out[: m.shape[0], : m.shape[1]] = m
    return out


ROW_AT = dict(r3=(0, 32), r1=(32, 128), r21=(160, 64), p1=(224, 128), p12=(352, 128), top=(480, 128))
COL_AT = dict(r1=(0, 256), r21=(256, 256), p1=(512, 128), p12=(640, 64))


def constants():
    row_maps, col_maps, col_top, col_res = [], [], [], []
    for v in range(3):
        r1, r2, p1, p2 = level_maps(ROWS, HALO, EXT, v)
        row_maps.append(
            np.concatenate(
                [
                    padded(own_to_top(ROWS, v), 32, 256),
                    padded(r1, 128, 256),
                    padded(r2 @ r1, 64, 256),
                    padded(p1, 128, 256),
                    padded(p1 @ p2, 128, 256),
                    padded(top_prolong(ROWS, 24, -1, v), 128, 256),
                ]
            )
        )
        r1, r2, p1, p2 = level_maps(TILE, MARGIN, WIN, v)
        col_maps.append(
            np.concatenate([r1.T, padded((r2 @ r1).T, 256, 128), p1.T, (p1 @ p2).T])
        )
        res = own_to_top(COLS, v)
        col_res.append(np.concatenate([res[8:136], res[136:144], np.zeros((112, COLS)), res[0:8]]).T)
        col_top.append(top_prolong(COLS, 144, -8, v).T)
    at = np.arange(512)
    sort = np.zeros((512, 512))
    sort[at, 128 * (at // 16 % 4) + 16 * (at // 64) + at % 16] = 1.0
    as_bf16 = lambda ms: np.stack(ms).astype(ml_dtypes.bfloat16)
    return as_bf16(row_maps), as_bf16(col_maps), as_bf16(col_res), as_bf16(col_top), as_bf16(sort)


def split(x):
    hi = x.astype(BF16)
    return hi, (x - hi.astype(F32)).astype(BF16)


def mm(a, b):
    return jnp.dot(a, b, preferred_element_type=F32)


def mm_right(a, b_h, b_l):
    return mm(jnp.concatenate([a, a], axis=1), jnp.concatenate([b_h, b_l], axis=0))


def mm_left(a_h, a_l, b):
    res = mm(jnp.concatenate([a_h, a_l], axis=0), b)
    return res[0 : a_h.shape[0]] + res[a_h.shape[0] :]


def mm_both(a_h, a_l, b_h, b_l):
    m, n = a_h.shape[0], b_h.shape[1]
    res = mm(jnp.concatenate([a_h, a_l], axis=0), jnp.concatenate([b_h, b_l], axis=1))
    return res[0:m, 0:n] + (res[0:m, n:] + res[m:, 0:n])


def mm_nt(a, b):
    return lax.dot_general(a, b, (((1,), (1,)), ((), ())), preferred_element_type=F32)


def band(shape, in_dim, shift, taps, level):
    chunks = []
    for start in range(0, shape[0], 64):
        part = (min(64, shape[0] - start), shape[1])
        row = lax.broadcasted_iota(jnp.int32, part, 0) + start
        col = lax.broadcasted_iota(jnp.int32, part, 1)
        d = (row - col if in_dim == 0 else col - row) + shift

        def place(k, m):
            return jnp.where(d == k, taps[level, k], m)

        chunks.append(lax.fori_loop(0, TAPS, place, jnp.zeros(part, F32)))
    return chunks[0] if len(chunks) == 1 else jnp.concatenate(chunks, axis=0)


def between(shape, dim, low, high):
    at = lax.broadcasted_iota(jnp.int32, shape, dim)
    return (at >= low) & (at < high)


def kernel(
    heat, taps_in, top_rows, top_cols, row_maps, col_maps, col_res, col_top, sort, out,
    taps, q, aw, to, ar, at, ab, bx, rmap, cmap, cres, ctop, perm,
    mr, y_hl, b_h, b_l, cm_w, es, nb, nb_mid, near_z, far_z, next_z, g, ps, pa, xb, acc,
    load_sem, rim_s, rim_r, halo_s, halo_r, aa_s, aa_r, ah_s, ah_r, bx_s, bx_r,
    z1_s, z1_r, z2_s, z2_r, pa_s, pa_r, xb_s, xb_r, out_s,
):
    w, n = lax.axis_index("wide"), lax.axis_index("narrow")
    z, qi = w // NQ, w % NQ
    y, xl = n // 2, n % 2

    def dev(dw, dn):
        return ((w + dw + NW) % NW, (n + dn + NN) % NN)

    def in_z(dz):
        return (((z + dz + NZ) % NZ) * NQ + qi, n)

    def in_row(k, dx):
        return (z * NQ + (qi + k + NQ) % NQ, 2 * y + (xl + dx) % 2)

    def in_y(dy):
        return (w, 2 * ((y + dy + NY) % NY) + xl)

    row_v = jnp.where(w == 0, 0, jnp.where(w == NW - 1, 2, 1))
    col_v = jnp.where(n == 0, 0, jnp.where(n == NN - 1, 2, 1))

    pairs = dict(
        heat=(heat, q.at[HALO : HALO + ROWS, SIDE : SIDE + COLS]),
        rows=(row_maps.at[row_v], rmap),
        res=(col_res.at[col_v], cres),
        top_rows=(top_rows, aw),
        sort=(sort, perm),
        top_cols=(top_cols, bx.at[8:136]),
        taps=(taps_in, taps),
        cols=(col_maps.at[1], cmap.at[0]),
        rim_cols=(col_maps.at[col_v], cmap.at[1]),
        top=(col_top.at[col_v], ctop),
    )
    loads = {
        name: pltpu.make_async_copy(src, dst, load_sem.at[i])
        for i, (name, (src, dst)) in enumerate(pairs.items())
    }
    for c in loads.values():
        c.start()

    barrier = pltpu.get_barrier_semaphore()
    around = [(dw, dn) for dw in (-1, 0, 1) for dn in (-1, 0, 1) if (dw, dn) != (0, 0)]
    greet = [dev(dw, dn) for dw, dn in around]
    hops = [(k, dx) for k in range(NQ) for dx in range(2) if (k, dx) != (0, 0)]
    greet += [in_row(-k, dx) for k, dx in hops]
    greet += [in_y(dy) for dy in (1, 2, 3)]
    greet += [in_z(dz) for dz in (1, -1, 3, -3, 6, -6, 8)]
    count = len(greet)
    greet += [(((z + NZ - 1) % NZ) * NQ + NQ - 1, n), (((z + 1) % NZ) * NQ, n)]
    for target in greet:
        pl.semaphore_signal(barrier, inc=1, device_id=target, device_id_type=MESH)

    def send(src, dst, send_sem, recv_sem, target):
        c = pltpu.make_async_remote_copy(
            src_ref=src, dst_ref=dst, send_sem=send_sem, recv_sem=recv_sem,
            device_id=target, device_id_type=MESH,
        )
        c.start()
        return c

    def rm(name, cols):
        start, rows = ROW_AT[name]
        return rmap[start : start + rows, 0:cols]

    own_rows = slice(HALO, HALO + ROWS)

    def strip(src, dst, i, target):
        return send(q.at[src], q.at[dst], halo_s.at[i], halo_r.at[i], target)

    loads["heat"].wait()
    loads["rows"].wait()
    loads["res"].wait()
    own_h, own_l = split(q[own_rows, SIDE : SIDE + COLS])
    r3 = rm("r3", ROWS)
    by_rows_h, by_rows_l = split(mm_right(r3, own_h, own_l))
    top = mm_left(by_rows_h, by_rows_l, cres[...])
    at_right = lax.broadcasted_iota(jnp.int32, (32, 128), 1) < 64
    es[:, 0:128] = jnp.where(at_right, 0.0, top[:, 128:256])
    es[:, 128:256] = top[:, 0:128]
    es[:, 256:384] = jnp.where(at_right, top[:, 128:256], 0.0)
    row_part = {-1: slice(0, 8), 0: slice(8, 24), 1: slice(24, 32)}
    col_part = {-1: slice(0, 128), 0: slice(128, 256), 1: slice(256, 384)}
    pl.semaphore_wait(barrier, jnp.where((qi == 0) | (qi == NQ - 1), count + NQ, count))
    rims = []
    for i, (dw, dn) in enumerate(around):
        dst = nb.at[i] if dw else nb_mid.at[i // 4]
        rims.append(
            send(es.at[row_part[dw], col_part[dn]], dst, rim_s.at[i], rim_r.at[i], dev(dw, dn))
        )

    strips = [
        strip((own_rows, slice(COLS, COLS + SIDE)), (own_rows, slice(0, SIDE)), 0, dev(0, 1)),
        strip((own_rows, slice(SIDE, 2 * SIDE)), (own_rows, slice(SIDE + COLS, WIDE)), 1, dev(0, -1)),
    ]

    loads["top_rows"].wait()
    loads["sort"].wait()
    halves = [split(aw[:, 512 * p : 512 * (p + 1)]) for p in range(2)]
    sorted_cols = mm(
        jnp.concatenate([halves[0][0], halves[1][0], halves[0][1], halves[1][1]], axis=0), perm[...]
    )
    sorted_cols = sorted_cols[0:32] + sorted_cols[32:64]
    for p in range(2):
        for k in range(NQ):
            to[k, p] = sorted_cols[16 * p : 16 * (p + 1), 128 * k : 128 * (k + 1)]
    plane = [
        send(to.at[(qi + k) % NQ], ar.at[qi], aa_s.at[k - 1], aa_r.at[k - 1], in_row(k, 0))
        for k in (1, 2, 3)
    ]
    ar[qi] = to[qi]

    def rim_copy(src, dst, side, p, dz):
        return pltpu.make_async_remote_copy(
            src_ref=src, dst_ref=dst, send_sem=ah_s.at[p], recv_sem=ah_r.at[side],
            device_id=(((z + dz + NZ) % NZ) * NQ + p, n), device_id_type=MESH,
        )

    def rim_down(p):
        return rim_copy(to.at[p, :, 8:16], at, 0, p, 1)

    def rim_up(p):
        return rim_copy(to.at[p, :, 0:8], ab, 1, p, -1)

    @pl.when(qi == NQ - 1)
    def _():
        for p in range(NQ):
            rim_down(p).start()

    @pl.when(qi == 0)
    def _():
        for p in range(NQ):
            rim_up(p).start()

    loads["top_cols"].wait()
    sides = [
        send(bx.at[128:136], bx.at[0:8], bx_s.at[0], bx_r.at[0], dev(0, 1)),
        send(bx.at[8:16], bx.at[136:144], bx_s.at[1], bx_r.at[1], dev(0, -1)),
    ]
    for c in rims:
        c.wait_recv()
    mid = nb_mid[0] + nb_mid[1]
    halves = [
        (es[8 + 8 * p : 16 + 8 * p, 128:256] + mid[8 * p : 8 * p + 8])
        + (nb[first] + (nb[first + 1] + nb[first + 2]))
        for p, first in ((0, 5), (1, 0))
    ]
    near_z[0] = jnp.concatenate(halves, axis=0)

    steps = (0, 3, -3, 6, -6)
    first_stage = [
        send(near_z.at[0], near_z.at[i], z1_s.at[i - 1], z1_r.at[i - 1], in_z(-steps[i]))
        for i in range(1, 5)
    ]
    first_stage.append(send(near_z.at[0], far_z, z1_s.at[4], z1_r.at[4], in_z(8)))

    for c in strips:
        c.wait_recv()
    outer = [
        strip(slice(ROWS, ROWS + HALO), slice(0, HALO), 2, dev(1, 0)),
        strip(slice(HALO, 2 * HALO), slice(HALO + ROWS, EXT), 3, dev(-1, 0)),
    ]

    loads["taps"].wait()

    low, high = jnp.where(w == 0, HALO, 0), jnp.where(w == NW - 1, HALO + ROWS, EXT)
    t0 = jnp.where(
        between((ROWS, EXT), 1, low, high), band((ROWS, EXT), 1, 8 - HALO, taps, 0), 0.0
    )

    def row_level(level, size, res, pro):
        th, tl = split(band((size, size), 1, 8, taps, level))
        tr_h, tr_l = split(mm_left(th, tl, res))
        return mm_right(pro, tr_h, tr_l)

    for i, m in enumerate(
        (t0, row_level(1, 128, rm("r1", EXT), rm("p1", 128)), row_level(2, 64, rm("r21", EXT), rm("p12", 64)))
    ):
        hi, lo = split(m)
        mr[i * ROWS : (i + 1) * ROWS, :] = hi
        mr[(i + 3) * ROWS : (i + 4) * ROWS, :] = lo

    def col_maps_of(i, low, high):
        def cm(name, cols):
            start, rows = COL_AT[name]
            return cmap[i, start : start + rows, 0:cols]

        maps = [
            jnp.where(
                between((WIN, TILE), 0, low, high),
                band((WIN, TILE), 0, 8 - MARGIN, taps, 0),
                0.0,
            )
        ]
        for level, size, res, pro in (
            (1, 128, cm("r1", 128), cm("p1", 128)),
            (2, 64, cm("r21", 64), cm("p12", 128)),
        ):
            th, tl = split(band((size, size), 0, 8, taps, level))
            tp_h, tp_l = split(mm_left(th, tl, pro))
            maps.append(mm_right(res, tp_h, tp_l))
        for t, m in enumerate(maps):
            hi, lo = split(m)
            cm_w[i, WIN * t : WIN * (t + 1), 0:TILE] = hi
            cm_w[i, WIN * t : WIN * (t + 1), TILE : 2 * TILE] = lo

    loads["cols"].wait()
    loads["rim_cols"].wait()

    @pl.loop(0, 2)
    def _(i):
        col_maps_of(
            i,
            jnp.where((i == 1) & (n == 0), MARGIN, 0),
            jnp.where((i == 1) & (n == NN - 1), MARGIN + TILE, WIN),
        )

    for c in plane:
        c.wait_recv()
    for side, dst in ((0, at), (1, ab)):
        rim_copy(dst, dst, side, 0, 1).wait_recv()
    blocks = [at] + [ar.at[k] for k in range(NQ)] + [ab]
    a_h, a_l = split(
        jnp.concatenate(
            [jnp.concatenate([b[0], b[1]], axis=1) for b in blocks], axis=0
        )
    )
    for c in sides:
        c.wait_recv()

    @pl.loop(0, COLS // 128)
    def _(j):
        at_j = pl.ds(pl.multiple_of(128 * j, 128), 128)
        b_h[:, at_j], b_l[:, at_j] = split(bx[:, at_j])

    loads["top"].wait()

    for c in first_stage[:4]:
        c.wait_recv()
    second_stage = [
        send(near_z, next_z.at[i], z2_s.at[i], z2_r.at[i], in_z(-dz)) for i, dz in enumerate((1, -1))
    ]
    for i, dz in enumerate(steps):
        g[(z + dz + NZ) % NZ] = near_z[i]
    first_stage[4].wait_recv()
    g[(z + 8) % NZ] = far_z[...]
    for k, on in enumerate((1, -1)):
        second_stage[k].wait_recv()
        for i, dz in enumerate(steps):
            g[(z + on + dz + NZ) % NZ] = next_z[k, i]
    g_h, g_l = split(g[...].reshape(256, 128))
    ps[...] = mm_both(a_h, a_l, g_h, g_l)

    partial_sums = []
    for i, (k, dx) in enumerate(hops):
        start = pl.multiple_of(16 * ((qi + k) % NQ), 16)
        partial_sums.append(
            send(ps.at[pl.ds(start, 32)], pa.at[xl, k], pa_s.at[i], pa_r.at[i], in_row(k, dx))
        )
    own = pl.multiple_of(16 * qi, 16)
    pa[xl, 0] = ps[pl.ds(own, 32), :]

    for c in outer:
        c.wait_recv()

    @pl.loop(0, SPAN // 128)
    def _(j):
        here = q[:, pl.ds(pl.multiple_of(128 * j, 128), 256)]
        hi, lo = split(pltpu.roll(here, 256 - MARGIN, 1)[:, 0:128])
        res = mm_both(mr[0 : 3 * ROWS], mr[3 * ROWS :], hi, lo)
        at_j = pl.ds(pl.multiple_of(128 * j, 128), 128)
        y_hl[0, :, at_j], y_hl[1, :, at_j] = split(res)

    for c in partial_sums:
        c.wait_recv()
    for b in range(2):
        total = (pa[b, 0] + pa[b, 1]) + (pa[b, 2] + pa[b, 3])
        xb[y, :, 128 * b : 128 * (b + 1)] = total[7:31, :]
    lines = [
        send(xb.at[y], xb.at[y], xb_s.at[k - 1], xb_r.at[k - 1], in_y(k)) for k in range(1, NY)
    ]

    @pl.loop(0, TILES)
    def _(j):
        at_rim = ((j == 0) & (n == 0)) | ((j == TILES - 1) & (n == NN - 1))
        at_j = pl.ds(pl.multiple_of(TILE * j, TILE), WIN)
        windows = [
            jnp.concatenate([y_hl[p, t * ROWS : (t + 1) * ROWS, at_j] for t in range(3)], axis=1)
            for p in range(2)
        ]
        both = mm(jnp.concatenate(windows, axis=0), cm_w[jnp.where(at_rim, 1, 0)])
        acc[:, pl.ds(pl.multiple_of(TILE * j, TILE), TILE)] = both[0:ROWS, 0:TILE] + (
            both[0:ROWS, TILE:] + both[ROWS:, 0:TILE]
        )

    for c in lines:
        c.wait_recv()
    lines_in = jnp.concatenate([xb[i] for i in range(NY)], axis=1)
    x_h, x_l = split(jnp.concatenate([lines_in, jnp.zeros((8, COLS), F32)], axis=0))
    with_hi = mm_nt(jnp.concatenate([x_h, x_l], axis=0), b_h[...])
    e_h, e_l = split(with_hi[0:32] + (with_hi[32:64] + mm_nt(x_h, b_l[...])))
    f_h, f_l = split(mm_left(e_h, e_l, ctop[...]))
    ur = rm("top", 32)
    pieces = []
    for i in range(4):
        at_i = slice(256 * i, 256 * (i + 1))
        acc[:, at_i] += mm_right(ur, f_h[:, at_i], f_l[:, at_i])
        pieces.append(pltpu.make_async_copy(acc.at[:, at_i], out.at[:, at_i], out_s.at[i]))
        pieces[-1].start()

    for c in rims + strips + plane + sides + outer + first_stage + second_stage + partial_sums + lines:
        c.wait_send()

    @pl.when(qi == NQ - 1)
    def _():
        for p in range(NQ):
            rim_down(p).wait_send()

    @pl.when(qi == 0)
    def _():
        for p in range(NQ):
            rim_up(p).wait_send()

    for c in pieces:
        c.wait()


def shards(maps, heat_power, level_taps, top_rows, top_cols):
    far_memory = pl.BlockSpec(memory_space=pltpu.HBM)
    sems = [10, 8, 8, 4, 4, 3, 3, 4, 2, 2, 2, 5, 5, 2, 2, 7, 7, 3, 3, 4]
    words = lambda *shape: pltpu.VMEM(shape, F32)
    halves = lambda *shape: pltpu.VMEM(shape, BF16)
    return pl.pallas_call(
        kernel,
        out_shape=jax.ShapeDtypeStruct((ROWS, COLS), F32),
        in_specs=[far_memory] * (4 + len(maps)),
        out_specs=far_memory,
        scratch_shapes=[
            pltpu.SMEM((3, TAPS), F32),
            words(EXT, WIDE),
            words(16, COLS),
            words(NQ, 2, 16, 128),
            words(NQ, 2, 16, 128),
            words(2, 8, 128),
            words(2, 8, 128),
            words(144, COLS),
            halves(*maps[0].shape[1:]),
            halves(2, *maps[1].shape[1:]),
            halves(*maps[2].shape[1:]),
            halves(*maps[3].shape[1:]),
            halves(*maps[4].shape),
            halves(6 * ROWS, EXT),
            halves(2, 3 * ROWS, SPAN),
            halves(144, COLS),
            halves(144, COLS),
            halves(2, 3 * WIN, 2 * TILE),
            words(32, 384),
            words(8, 8, 128),
            words(2, 16, 128),
            words(5, 16, 128),
            words(16, 128),
            words(2, 5, 16, 128),
            words(NZ, 16, 128),
            words(80, 128),
            words(2, NQ, 32, 128),
            words(NY, 24, 256),
            words(ROWS, COLS),
        ]
        + [pltpu.SemaphoreType.DMA((k,)) for k in sems],
        compiler_params=pltpu.CompilerParams(
            collective_id=0, has_side_effects=True, vmem_limit_bytes=62 * 1024 * 1024
        ),
    )(heat_power, level_taps, top_rows, top_cols, *maps)


def solution(mesh):
    maps = constants()
    return jax.shard_map(
        functools.partial(shards, maps),
        mesh=mesh,
        in_specs=(P("wide", "narrow"), P(), P("wide", None), P("narrow", None)),
        out_specs=P("wide", "narrow"),
        check_vma=False,
    )
```

```python
import functools

import jax
import jax.numpy as jnp
import ml_dtypes
import numpy as np
from jax import lax
from jax.experimental import pallas as pl
from jax.experimental.pallas import tpu as pltpu
from jax.sharding import PartitionSpec as P

F32 = jnp.float32
BF16 = jnp.bfloat16
MESH = pl.DeviceIdType.MESH
TAPS = 17
NZ, NQ, NN, NY = 16, 4, 8, 4
NW = NZ * NQ
ROWS, COLS = 128, 1024
HALO = 40
EXT = ROWS + 2 * HALO
SIDE = 128
WIDE = COLS + 2 * SIDE
TILE = 128
MARGIN = 64
WIN = TILE + 2 * MARGIN
SPAN = COLS + 2 * MARGIN
TILES = COLS // TILE


def restriction(out_n, out_off, in_n, in_off, first, out_end, in_end):
    out_at = np.arange(out_n)[:, None] + out_off
    in_at = np.arange(in_n)[None, :] + in_off
    d = in_at - 2 * out_at
    m = np.where((d == 0) | (d == 1), 0.375, 0.0) + np.where((d == -1) | (d == 2), 0.125, 0.0)
    if first:
        m = np.where((out_at >= 0) & (in_at >= 0), m, 0.0)
    if out_end is not None:
        m = np.where((out_at < out_end) & (in_at < in_end), m, 0.0)
    return m


def prolongation(out_n, out_off, in_n, in_off, first, in_end):
    out_at = np.arange(out_n)[:, None] + out_off
    in_at = np.arange(in_n)[None, :] + in_off
    d = out_at - 2 * in_at
    m = np.where((d == 0) | (d == 1), 0.75, 0.0) + np.where((d == -1) | (d == 2), 0.25, 0.0)
    if first:
        m = np.where(in_at >= 0, m, 0.0)
    if in_end is not None:
        m = np.where(in_at < in_end, m, 0.0)
    return m


def level_maps(block, off, size, variant):
    first, last = variant == 0, variant == 2
    end = [block >> t if last else None for t in range(4)]
    r1 = restriction(size // 2, -off // 2, size, -off, first, end[1], end[0])
    r2 = restriction(size // 4, -off // 4, size // 2, -off // 2, first, end[2], end[1])
    p1 = prolongation(block, 0, size // 2, -off // 2, first, end[1])
    p2 = prolongation(size // 2, -off // 2, size // 4, -off // 4, first, end[2])
    return r1, r2, p1, p2


def top_prolong(block, in_n, in_off, variant):
    first, last = variant == 0, variant == 2
    end = [block >> t if last else None for t in range(4)]
    p3 = prolongation(block // 4 + 4, -2, in_n, in_off, first, end[3])
    p2 = prolongation(block // 2 + 4, -2, block // 4 + 4, -2, first, end[2])
    p1 = prolongation(block, 0, block // 2 + 4, -2, first, end[1])
    return p1 @ p2 @ p3


def own_to_top(block, variant):
    first, last = variant == 0, variant == 2
    end = [block >> t if last else None for t in range(4)]
    r1 = restriction(block // 2 + 16, -8, block, 0, first, end[1], end[0])
    r2 = restriction(block // 4 + 16, -8, block // 2 + 16, -8, first, end[2], end[1])
    r3 = restriction(block // 8 + 16, -8, block // 4 + 16, -8, first, end[3], end[2])
    return r3 @ r2 @ r1


def padded(m, rows, cols):
    out = np.zeros((rows, cols))
    out[: m.shape[0], : m.shape[1]] = m
    return out


ROW_AT = dict(r3=(0, 32), r1=(32, 128), r21=(160, 64), p1=(224, 128), p12=(352, 128), top=(480, 128))
COL_AT = dict(r1=(0, 256), r21=(256, 256), p1=(512, 128), p12=(640, 64))


def constants():
    row_maps, col_maps, col_top, col_res = [], [], [], []
    for v in range(3):
        r1, r2, p1, p2 = level_maps(ROWS, HALO, EXT, v)
        row_maps.append(
            np.concatenate(
                [
                    padded(own_to_top(ROWS, v), 32, 256),
                    padded(r1, 128, 256),
                    padded(r2 @ r1, 64, 256),
                    padded(p1, 128, 256),
                    padded(p1 @ p2, 128, 256),
                    padded(top_prolong(ROWS, 24, -1, v), 128, 256),
                ]
            )
        )
        r1, r2, p1, p2 = level_maps(TILE, MARGIN, WIN, v)
        col_maps.append(
            np.concatenate([r1.T, padded((r2 @ r1).T, 256, 128), p1.T, (p1 @ p2).T])
        )
        res = own_to_top(COLS, v)
        col_res.append(np.concatenate([res[8:136], res[136:144], np.zeros((112, COLS)), res[0:8]]).T)
        col_top.append(top_prolong(COLS, 144, -8, v).T)
    at = np.arange(512)
    sort = np.zeros((512, 512))
    sort[at, 128 * (at // 16 % 4) + 16 * (at // 64) + at % 16] = 1.0
    as_bf16 = lambda ms: np.stack(ms).astype(ml_dtypes.bfloat16)
    return as_bf16(row_maps), as_bf16(col_maps), as_bf16(col_res), as_bf16(col_top), as_bf16(sort)


def split(x):
    hi = x.astype(BF16)
    return hi, (x - hi.astype(F32)).astype(BF16)


def mm(a, b):
    return jnp.dot(a, b, preferred_element_type=F32)


def mm_right(a, b_h, b_l):
    return mm(jnp.concatenate([a, a], axis=1), jnp.concatenate([b_h, b_l], axis=0))


def mm_left(a_h, a_l, b):
    res = mm(jnp.concatenate([a_h, a_l], axis=0), b)
    return res[0 : a_h.shape[0]] + res[a_h.shape[0] :]


def mm_both(a_h, a_l, b_h, b_l):
    m, n = a_h.shape[0], b_h.shape[1]
    res = mm(jnp.concatenate([a_h, a_l], axis=0), jnp.concatenate([b_h, b_l], axis=1))
    return res[0:m, 0:n] + (res[0:m, n:] + res[m:, 0:n])


def mm_nt(a, b):
    return lax.dot_general(a, b, (((1,), (1,)), ((), ())), preferred_element_type=F32)


def band(shape, in_dim, shift, taps, level):
    chunks = []
    for start in range(0, shape[0], 64):
        part = (min(64, shape[0] - start), shape[1])
        row = lax.broadcasted_iota(jnp.int32, part, 0) + start
        col = lax.broadcasted_iota(jnp.int32, part, 1)
        d = (row - col if in_dim == 0 else col - row) + shift

        def place(k, m):
            return jnp.where(d == k, taps[level, k], m)

        chunks.append(lax.fori_loop(0, TAPS, place, jnp.zeros(part, F32)))
    return chunks[0] if len(chunks) == 1 else jnp.concatenate(chunks, axis=0)


def between(shape, dim, low, high):
    at = lax.broadcasted_iota(jnp.int32, shape, dim)
    return (at >= low) & (at < high)


def kernel(
    heat, taps_in, top_rows, top_cols, row_maps, col_maps, col_res, col_top, sort, out,
    taps, q, aw, to, ar, at, ab, bx, rmap, cmap, cres, ctop, perm,
    mr, y_hl, b_h, b_l, cm_w, es, nb, nb_mid, g, ps, pa, xb, acc,
    load_sem, rim_s, rim_r, halo_s, halo_r, aa_s, aa_r, ah_s, ah_r, bx_s, bx_r,
    z_s, z_r, pa_s, pa_r, xb_s, xb_r, out_s,
):
    w, n = lax.axis_index("wide"), lax.axis_index("narrow")
    z, qi = w // NQ, w % NQ
    y, xl = n // 2, n % 2

    def dev(dw, dn):
        return ((w + dw + NW) % NW, (n + dn + NN) % NN)

    def in_z(dz):
        return (((z + dz + NZ) % NZ) * NQ + qi, n)

    def in_row(k, dx):
        return (z * NQ + (qi + k + NQ) % NQ, 2 * y + (xl + dx) % 2)

    def in_y(dy):
        return (w, 2 * ((y + dy + NY) % NY) + xl)

    row_v = jnp.where(w == 0, 0, jnp.where(w == NW - 1, 2, 1))
    col_v = jnp.where(n == 0, 0, jnp.where(n == NN - 1, 2, 1))

    pairs = dict(
        heat=(heat, q.at[HALO : HALO + ROWS, SIDE : SIDE + COLS]),
        rows=(row_maps.at[row_v], rmap),
        res=(col_res.at[col_v], cres),
        top_rows=(top_rows, aw),
        sort=(sort, perm),
        top_cols=(top_cols, bx.at[8:136]),
        taps=(taps_in, taps),
        cols=(col_maps.at[1], cmap.at[0]),
        rim_cols=(col_maps.at[col_v], cmap.at[1]),
        top=(col_top.at[col_v], ctop),
    )
    loads = {
        name: pltpu.make_async_copy(src, dst, load_sem.at[i])
        for i, (name, (src, dst)) in enumerate(pairs.items())
    }
    for name in ("heat", "rows", "res"):
        loads[name].start()

    barrier = pltpu.get_barrier_semaphore()
    around = [(dw, dn) for dw in (-1, 0, 1) for dn in (-1, 0, 1) if (dw, dn) != (0, 0)]
    greet = [dev(dw, dn) for dw, dn in around]
    hops = [(k, dx) for k in range(NQ) for dx in range(2) if (k, dx) != (0, 0)]
    greet += [in_row(-k, dx) for k, dx in hops]
    greet += [in_y(dy) for dy in (1, 2, 3)]
    along = [8] + [d for dz in range(7, 0, -1) for d in (dz, -dz)]
    greet += [in_z(dz) for dz in along]
    count = len(greet)
    greet += [(((z + NZ - 1) % NZ) * NQ + NQ - 1, n), (((z + 1) % NZ) * NQ, n)]
    for target in greet:
        pl.semaphore_signal(barrier, inc=1, device_id=target, device_id_type=MESH)
    for name in ("top_rows", "sort", "top_cols", "taps", "cols", "rim_cols", "top"):
        loads[name].start()

    def send(src, dst, send_sem, recv_sem, target):
        c = pltpu.make_async_remote_copy(
            src_ref=src, dst_ref=dst, send_sem=send_sem, recv_sem=recv_sem,
            device_id=target, device_id_type=MESH,
        )
        c.start()
        return c

    def rm(name, cols):
        start, rows = ROW_AT[name]
        return rmap[start : start + rows, 0:cols]

    own_rows = slice(HALO, HALO + ROWS)

    def strip(src, dst, i, target):
        return send(q.at[src], q.at[dst], halo_s.at[i], halo_r.at[i], target)

    loads["heat"].wait()
    loads["rows"].wait()
    loads["res"].wait()
    own_h, own_l = split(q[own_rows, SIDE : SIDE + COLS])
    r3 = rm("r3", ROWS)
    by_rows_h, by_rows_l = split(mm_right(r3, own_h, own_l))
    top = mm_left(by_rows_h, by_rows_l, cres[...])
    at_right = lax.broadcasted_iota(jnp.int32, (32, 128), 1) < 64
    es[:, 0:128] = jnp.where(at_right, 0.0, top[:, 128:256])
    es[:, 128:256] = top[:, 0:128]
    es[:, 256:384] = jnp.where(at_right, top[:, 128:256], 0.0)
    row_part = {-1: slice(0, 8), 0: slice(8, 24), 1: slice(24, 32)}
    col_part = {-1: slice(0, 128), 0: slice(128, 256), 1: slice(256, 384)}
    pl.semaphore_wait(barrier, jnp.where((qi == 0) | (qi == NQ - 1), count + NQ, count))
    rims = []
    for i, (dw, dn) in enumerate(around):
        dst = nb.at[i] if dw else nb_mid.at[i // 4]
        rims.append(
            send(es.at[row_part[dw], col_part[dn]], dst, rim_s.at[i], rim_r.at[i], dev(dw, dn))
        )

    strips = [
        strip((own_rows, slice(COLS, COLS + SIDE)), (own_rows, slice(0, SIDE)), 0, dev(0, 1)),
        strip((own_rows, slice(SIDE, 2 * SIDE)), (own_rows, slice(SIDE + COLS, WIDE)), 1, dev(0, -1)),
    ]

    loads["top_rows"].wait()
    loads["sort"].wait()
    halves = [split(aw[:, 512 * p : 512 * (p + 1)]) for p in range(2)]
    sorted_cols = mm(
        jnp.concatenate([halves[0][0], halves[1][0], halves[0][1], halves[1][1]], axis=0), perm[...]
    )
    sorted_cols = sorted_cols[0:32] + sorted_cols[32:64]
    for p in range(2):
        for k in range(NQ):
            to[k, p] = sorted_cols[16 * p : 16 * (p + 1), 128 * k : 128 * (k + 1)]
    plane = [
        send(to.at[(qi + k) % NQ], ar.at[qi], aa_s.at[k - 1], aa_r.at[k - 1], in_row(k, 0))
        for k in (1, 2, 3)
    ]
    ar[qi] = to[qi]

    def rim_copy(src, dst, side, p, dz):
        return pltpu.make_async_remote_copy(
            src_ref=src, dst_ref=dst, send_sem=ah_s.at[p], recv_sem=ah_r.at[side],
            device_id=(((z + dz + NZ) % NZ) * NQ + p, n), device_id_type=MESH,
        )

    def rim_down(p):
        return rim_copy(to.at[p, :, 8:16], at, 0, p, 1)

    def rim_up(p):
        return rim_copy(to.at[p, :, 0:8], ab, 1, p, -1)

    @pl.when(qi == NQ - 1)
    def _():
        for p in range(NQ):
            rim_down(p).start()

    @pl.when(qi == 0)
    def _():
        for p in range(NQ):
            rim_up(p).start()

    loads["top_cols"].wait()
    sides = [
        send(bx.at[128:136], bx.at[0:8], bx_s.at[0], bx_r.at[0], dev(0, 1)),
        send(bx.at[8:16], bx.at[136:144], bx_s.at[1], bx_r.at[1], dev(0, -1)),
    ]
    for c in strips:
        c.wait_recv()
    outer = [
        strip(slice(ROWS, ROWS + HALO), slice(0, HALO), 2, dev(1, 0)),
        strip(slice(HALO, 2 * HALO), slice(HALO + ROWS, EXT), 3, dev(-1, 0)),
    ]

    for c in rims:
        c.wait_recv()
    mid = nb_mid[0] + nb_mid[1]
    halves = [
        (es[8 + 8 * p : 16 + 8 * p, 128:256] + mid[8 * p : 8 * p + 8])
        + (nb[first] + (nb[first + 1] + nb[first + 2]))
        for p, first in ((0, 5), (1, 0))
    ]
    g[z] = jnp.concatenate(halves, axis=0)

    column = [
        send(g.at[z], g.at[z], z_s.at[i], z_r.at[i], in_z(dz)) for i, dz in enumerate(along)
    ]

    loads["taps"].wait()

    low, high = jnp.where(w == 0, HALO, 0), jnp.where(w == NW - 1, HALO + ROWS, EXT)
    t0 = jnp.where(
        between((ROWS, EXT), 1, low, high), band((ROWS, EXT), 1, 8 - HALO, taps, 0), 0.0
    )

    def row_level(level, size, res, pro):
        th, tl = split(band((size, size), 1, 8, taps, level))
        tr_h, tr_l = split(mm_left(th, tl, res))
        return mm_right(pro, tr_h, tr_l)

    for i, m in enumerate(
        (t0, row_level(1, 128, rm("r1", EXT), rm("p1", 128)), row_level(2, 64, rm("r21", EXT), rm("p12", 64)))
    ):
        hi, lo = split(m)
        mr[i * ROWS : (i + 1) * ROWS, :] = hi
        mr[(i + 3) * ROWS : (i + 4) * ROWS, :] = lo

    def col_maps_of(i, low, high):
        def cm(name, cols):
            start, rows = COL_AT[name]
            return cmap[i, start : start + rows, 0:cols]

        maps = [
            jnp.where(
                between((WIN, TILE), 0, low, high),
                band((WIN, TILE), 0, 8 - MARGIN, taps, 0),
                0.0,
            )
        ]
        for level, size, res, pro in (
            (1, 128, cm("r1", 128), cm("p1", 128)),
            (2, 64, cm("r21", 64), cm("p12", 128)),
        ):
            th, tl = split(band((size, size), 0, 8, taps, level))
            tp_h, tp_l = split(mm_left(th, tl, pro))
            maps.append(mm_right(res, tp_h, tp_l))
        for t, m in enumerate(maps):
            hi, lo = split(m)
            cm_w[i, WIN * t : WIN * (t + 1), 0:TILE] = hi
            cm_w[i, WIN * t : WIN * (t + 1), TILE : 2 * TILE] = lo

    loads["cols"].wait()
    loads["rim_cols"].wait()

    @pl.loop(0, 2)
    def _(i):
        col_maps_of(
            i,
            jnp.where((i == 1) & (n == 0), MARGIN, 0),
            jnp.where((i == 1) & (n == NN - 1), MARGIN + TILE, WIN),
        )

    for c in plane:
        c.wait_recv()
    for side, dst in ((0, at), (1, ab)):
        rim_copy(dst, dst, side, 0, 1).wait_recv()
    blocks = [at] + [ar.at[k] for k in range(NQ)] + [ab]
    a_h, a_l = split(
        jnp.concatenate(
            [jnp.concatenate([b[0], b[1]], axis=1) for b in blocks], axis=0
        )
    )
    for c in sides:
        c.wait_recv()

    @pl.loop(0, COLS // 128)
    def _(j):
        at_j = pl.ds(pl.multiple_of(128 * j, 128), 128)
        b_h[:, at_j], b_l[:, at_j] = split(bx[:, at_j])

    loads["top"].wait()

    for c in column:
        c.wait_recv()
    g_h, g_l = split(g[...].reshape(256, 128))
    ps[...] = mm_both(a_h, a_l, g_h, g_l)

    partial_sums = []
    for i, (k, dx) in enumerate(hops):
        start = pl.multiple_of(16 * ((qi + k) % NQ), 16)
        partial_sums.append(
            send(ps.at[pl.ds(start, 32)], pa.at[xl, k], pa_s.at[i], pa_r.at[i], in_row(k, dx))
        )
    own = pl.multiple_of(16 * qi, 16)
    pa[xl, 0] = ps[pl.ds(own, 32), :]

    for c in outer:
        c.wait_recv()

    @pl.loop(0, SPAN // 128)
    def _(j):
        here = q[:, pl.ds(pl.multiple_of(128 * j, 128), 256)]
        hi, lo = split(pltpu.roll(here, 256 - MARGIN, 1)[:, 0:128])
        res = mm_both(mr[0 : 3 * ROWS], mr[3 * ROWS :], hi, lo)
        at_j = pl.ds(pl.multiple_of(128 * j, 128), 128)
        y_hl[0, :, at_j], y_hl[1, :, at_j] = split(res)

    for c in partial_sums:
        c.wait_recv()
    for b in range(2):
        total = (pa[b, 0] + pa[b, 1]) + (pa[b, 2] + pa[b, 3])
        xb[y, :, 128 * b : 128 * (b + 1)] = total[7:31, :]
    lines = [
        send(xb.at[y], xb.at[y], xb_s.at[k - 1], xb_r.at[k - 1], in_y(k)) for k in range(1, NY)
    ]

    @pl.loop(0, TILES)
    def _(j):
        at_rim = ((j == 0) & (n == 0)) | ((j == TILES - 1) & (n == NN - 1))
        at_j = pl.ds(pl.multiple_of(TILE * j, TILE), WIN)
        windows = [
            jnp.concatenate([y_hl[p, t * ROWS : (t + 1) * ROWS, at_j] for t in range(3)], axis=1)
            for p in range(2)
        ]
        both = mm(jnp.concatenate(windows, axis=0), cm_w[jnp.where(at_rim, 1, 0)])
        acc[:, pl.ds(pl.multiple_of(TILE * j, TILE), TILE)] = both[0:ROWS, 0:TILE] + (
            both[0:ROWS, TILE:] + both[ROWS:, 0:TILE]
        )

    for c in lines:
        c.wait_recv()
    lines_in = jnp.concatenate([xb[i] for i in range(NY)], axis=1)
    x_h, x_l = split(jnp.concatenate([lines_in, jnp.zeros((8, COLS), F32)], axis=0))
    with_hi = mm_nt(jnp.concatenate([x_h, x_l], axis=0), b_h[...])
    e_h, e_l = split(with_hi[0:32] + (with_hi[32:64] + mm_nt(x_h, b_l[...])))
    f_h, f_l = split(mm_left(e_h, e_l, ctop[...]))
    ur = rm("top", 32)
    pieces = []
    for i in range(4):
        at_i = slice(256 * i, 256 * (i + 1))
        acc[:, at_i] += mm_right(ur, f_h[:, at_i], f_l[:, at_i])
        pieces.append(pltpu.make_async_copy(acc.at[:, at_i], out.at[:, at_i], out_s.at[i]))
        pieces[-1].start()

    for c in rims + strips + plane + sides + outer + column + partial_sums + lines:
        c.wait_send()

    @pl.when(qi == NQ - 1)
    def _():
        for p in range(NQ):
            rim_down(p).wait_send()

    @pl.when(qi == 0)
    def _():
        for p in range(NQ):
            rim_up(p).wait_send()

    for c in pieces:
        c.wait()


def shards(maps, heat_power, level_taps, top_rows, top_cols):
    far_memory = pl.BlockSpec(memory_space=pltpu.HBM)
    sems = [10, 8, 8, 4, 4, 3, 3, 4, 2, 2, 2, 15, 15, 7, 7, 3, 3, 4]
    words = lambda *shape: pltpu.VMEM(shape, F32)
    halves = lambda *shape: pltpu.VMEM(shape, BF16)
    return pl.pallas_call(
        kernel,
        out_shape=jax.ShapeDtypeStruct((ROWS, COLS), F32),
        in_specs=[far_memory] * (4 + len(maps)),
        out_specs=far_memory,
        scratch_shapes=[
            pltpu.SMEM((3, TAPS), F32),
            words(EXT, WIDE),
            words(16, COLS),
            words(NQ, 2, 16, 128),
            words(NQ, 2, 16, 128),
            words(2, 8, 128),
            words(2, 8, 128),
            words(144, COLS),
            halves(*maps[0].shape[1:]),
            halves(2, *maps[1].shape[1:]),
            halves(*maps[2].shape[1:]),
            halves(*maps[3].shape[1:]),
            halves(*maps[4].shape),
            halves(6 * ROWS, EXT),
            halves(2, 3 * ROWS, SPAN),
            halves(144, COLS),
            halves(144, COLS),
            halves(2, 3 * WIN, 2 * TILE),
            words(32, 384),
            words(8, 8, 128),
            words(2, 16, 128),
            words(NZ, 16, 128),
            words(80, 128),
            words(2, NQ, 32, 128),
            words(NY, 24, 256),
            words(ROWS, COLS),
        ]
        + [pltpu.SemaphoreType.DMA((k,)) for k in sems],
        compiler_params=pltpu.CompilerParams(
            collective_id=0, has_side_effects=True, vmem_limit_bytes=62 * 1024 * 1024
        ),
    )(heat_power, level_taps, top_rows, top_cols, *maps)


def solution(mesh):
    maps = constants()
    return jax.shard_map(
        functools.partial(shards, maps),
        mesh=mesh,
        in_specs=(P("wide", "narrow"), P(), P("wide", None), P("narrow", None)),
        out_specs=P("wide", "narrow"),
        check_vma=False,
    )
```

```python
import functools

import jax
import jax.numpy as jnp
import ml_dtypes
import numpy as np
from jax import lax
from jax.experimental import pallas as pl
from jax.experimental.pallas import tpu as pltpu
from jax.sharding import PartitionSpec as P

F32 = jnp.float32
BF16 = jnp.bfloat16
MESH = pl.DeviceIdType.MESH
TAPS = 17
NZ, NQ, NN, NY = 16, 4, 8, 4
NW = NZ * NQ
ROWS, COLS = 128, 1024
HALO = 40
EXT = ROWS + 2 * HALO
DEEP = 256
SIDE = 128
WIDE = COLS + 2 * SIDE
TILE = 128
MARGIN = 64
WIN = TILE + 2 * MARGIN
SPAN = COLS + 2 * MARGIN
TILES = COLS // TILE


def restriction(out_n, out_off, in_n, in_off, first, out_end, in_end):
    out_at = np.arange(out_n)[:, None] + out_off
    in_at = np.arange(in_n)[None, :] + in_off
    d = in_at - 2 * out_at
    m = np.where((d == 0) | (d == 1), 0.375, 0.0) + np.where((d == -1) | (d == 2), 0.125, 0.0)
    if first:
        m = np.where((out_at >= 0) & (in_at >= 0), m, 0.0)
    if out_end is not None:
        m = np.where((out_at < out_end) & (in_at < in_end), m, 0.0)
    return m


def prolongation(out_n, out_off, in_n, in_off, first, in_end):
    out_at = np.arange(out_n)[:, None] + out_off
    in_at = np.arange(in_n)[None, :] + in_off
    d = out_at - 2 * in_at
    m = np.where((d == 0) | (d == 1), 0.75, 0.0) + np.where((d == -1) | (d == 2), 0.25, 0.0)
    if first:
        m = np.where(in_at >= 0, m, 0.0)
    if in_end is not None:
        m = np.where(in_at < in_end, m, 0.0)
    return m


def level_maps(block, off, size, variant):
    first, last = variant == 0, variant == 2
    end = [block >> t if last else None for t in range(4)]
    r1 = restriction(size // 2, -off // 2, size, -off, first, end[1], end[0])
    r2 = restriction(size // 4, -off // 4, size // 2, -off // 2, first, end[2], end[1])
    p1 = prolongation(block, 0, size // 2, -off // 2, first, end[1])
    p2 = prolongation(size // 2, -off // 2, size // 4, -off // 4, first, end[2])
    return r1, r2, p1, p2


def top_prolong(block, in_n, in_off, variant):
    first, last = variant == 0, variant == 2
    end = [block >> t if last else None for t in range(4)]
    p3 = prolongation(block // 4 + 4, -2, in_n, in_off, first, end[3])
    p2 = prolongation(block // 2 + 4, -2, block // 4 + 4, -2, first, end[2])
    p1 = prolongation(block, 0, block // 2 + 4, -2, first, end[1])
    return p1 @ p2 @ p3


def own_to_top(block, variant):
    first, last = variant == 0, variant == 2
    end = [block >> t if last else None for t in range(4)]
    r1 = restriction(block // 2 + 16, -8, block, 0, first, end[1], end[0])
    r2 = restriction(block // 4 + 16, -8, block // 2 + 16, -8, first, end[2], end[1])
    r3 = restriction(block // 8 + 16, -8, block // 4 + 16, -8, first, end[3], end[2])
    return r3 @ r2 @ r1


def padded(m, rows, cols):
    out = np.zeros((rows, cols))
    out[: m.shape[0], : m.shape[1]] = m
    return out


ROW_AT = dict(r3=(0, 32), r1=(32, 128), r21=(160, 64), p1=(224, 128), p12=(352, 128), top=(480, 128))
COL_AT = dict(r1=(0, 256), r21=(256, 256), p1=(512, 128), p12=(640, 64))


def constants():
    row_maps, col_maps, col_top, col_res = [], [], [], []
    for v in range(3):
        r1, r2, p1, p2 = level_maps(ROWS, HALO, EXT, v)
        row_maps.append(
            np.concatenate(
                [
                    padded(own_to_top(ROWS, v), 32, 256),
                    padded(r1, 128, 256),
                    padded(r2 @ r1, 64, 256),
                    padded(p1, 128, 256),
                    padded(p1 @ p2, 128, 256),
                    padded(top_prolong(ROWS, 24, -1, v), 128, 256),
                ]
            )
        )
        r1, r2, p1, p2 = level_maps(TILE, MARGIN, WIN, v)
        col_maps.append(
            np.concatenate([r1.T, padded((r2 @ r1).T, 256, 128), p1.T, (p1 @ p2).T])
        )
        res = own_to_top(COLS, v)
        col_res.append(np.concatenate([res[8:136], res[136:144], np.zeros((112, COLS)), res[0:8]]).T)
        col_top.append(top_prolong(COLS, 144, -8, v).T)
    at = np.arange(512)
    sort = np.zeros((512, 512))
    sort[at, 128 * (at // 16 % 4) + 16 * (at // 64) + at % 16] = 1.0
    as_bf16 = lambda ms: np.stack(ms).astype(ml_dtypes.bfloat16)
    return as_bf16(row_maps), as_bf16(col_maps), as_bf16(col_res), as_bf16(col_top), as_bf16(sort)


def split(x):
    hi = x.astype(BF16)
    return hi, (x - hi.astype(F32)).astype(BF16)


def mm(a, b):
    return jnp.dot(a, b, preferred_element_type=F32)


def mm_right(a, b_h, b_l):
    return mm(jnp.concatenate([a, a], axis=1), jnp.concatenate([b_h, b_l], axis=0))


def mm_left(a_h, a_l, b):
    res = mm(jnp.concatenate([a_h, a_l], axis=0), b)
    return res[0 : a_h.shape[0]] + res[a_h.shape[0] :]


def mm_both(a_h, a_l, b_h, b_l):
    m, n = a_h.shape[0], b_h.shape[1]
    res = mm(jnp.concatenate([a_h, a_l], axis=0), jnp.concatenate([b_h, b_l], axis=1))
    return res[0:m, 0:n] + (res[0:m, n:] + res[m:, 0:n])


def mm_nt(a, b):
    return lax.dot_general(a, b, (((1,), (1,)), ((), ())), preferred_element_type=F32)


def band(shape, in_dim, shift, taps, level):
    row = lax.broadcasted_iota(jnp.int32, (8, 256), 0)
    col = lax.broadcasted_iota(jnp.int32, (8, 256), 1)
    d = ((row - col if in_dim == 0 else col - row) + shift + 512) & 255
    first = jnp.zeros((8, 256), F32)
    for k in range(TAPS):
        first = jnp.where(d == k, taps[level, k], first)
    parts = [first] + [pltpu.roll(first, at, 1) for at in range(8, shape[0], 8)]
    return jnp.concatenate([p[:, 0 : shape[1]] for p in parts], axis=0)


def between(shape, dim, low, high):
    at = lax.broadcasted_iota(jnp.int32, shape, dim)
    return (at >= low) & (at < high)


def kernel(
    heat, taps_in, top_rows, top_cols, row_maps, col_maps, col_res, col_top, sort, out,
    taps, q, aw, to, ar, at, ab, bx, rmap, cmap, cres, ctop, perm,
    mr, y_hl, b_h, b_l, cm_w, es, nb, nb_mid, g, ps, pa, xb, acc,
    load_sem, rim_s, rim_r, halo_s, halo_r, aa_s, aa_r, ah_s, ah_r, bx_s, bx_r,
    z_s, z_r, pa_s, pa_r, xb_s, xb_r, out_s,
):
    w, n = lax.axis_index("wide"), lax.axis_index("narrow")
    z, qi = w // NQ, w % NQ
    y, xl = n // 2, n % 2

    def dev(dw, dn):
        return ((w + dw + NW) % NW, (n + dn + NN) % NN)

    def in_z(dz):
        return (((z + dz + NZ) % NZ) * NQ + qi, n)

    def in_row(k, dx):
        return (z * NQ + (qi + k + NQ) % NQ, 2 * y + (xl + dx) % 2)

    def in_y(dy):
        return (w, 2 * ((y + dy + NY) % NY) + xl)

    row_v = jnp.where(w == 0, 0, jnp.where(w == NW - 1, 2, 1))
    col_v = jnp.where(n == 0, 0, jnp.where(n == NN - 1, 2, 1))

    pairs = dict(
        heat=(heat, q.at[HALO : HALO + ROWS, SIDE : SIDE + COLS]),
        rows=(row_maps.at[row_v], rmap),
        res=(col_res.at[col_v], cres),
        top_rows=(top_rows, aw),
        sort=(sort, perm),
        top_cols=(top_cols, bx.at[8:136]),
        taps=(taps_in, taps),
        cols=(col_maps.at[1], cmap.at[0]),
        rim_cols=(col_maps.at[col_v], cmap.at[1]),
        top=(col_top.at[col_v], ctop),
    )
    loads = {
        name: pltpu.make_async_copy(src, dst, load_sem.at[i])
        for i, (name, (src, dst)) in enumerate(pairs.items())
    }
    for name in ("heat", "rows", "res"):
        loads[name].start()

    barrier = pltpu.get_barrier_semaphore()
    around = [(dw, dn) for dw in (-1, 0, 1) for dn in (-1, 0, 1) if (dw, dn) != (0, 0)]
    greet = [dev(dw, dn) for dw, dn in around]
    hops = [(k, dx) for k in range(NQ) for dx in range(2) if (k, dx) != (0, 0)]
    greet += [in_row(-k, dx) for k, dx in hops]
    greet += [in_y(dy) for dy in (1, 2, 3)]
    along = [8] + [d for dz in range(7, 0, -1) for d in (dz, -dz)]
    greet += [in_z(dz) for dz in along]
    count = len(greet)
    greet += [(((z + NZ - 1) % NZ) * NQ + NQ - 1, n), (((z + 1) % NZ) * NQ, n)]
    for target in greet:
        pl.semaphore_signal(barrier, inc=1, device_id=target, device_id_type=MESH)
    for name in ("top_rows", "sort", "top_cols", "taps", "cols", "rim_cols", "top"):
        loads[name].start()

    def send(src, dst, send_sem, recv_sem, target):
        c = pltpu.make_async_remote_copy(
            src_ref=src, dst_ref=dst, send_sem=send_sem, recv_sem=recv_sem,
            device_id=target, device_id_type=MESH,
        )
        c.start()
        return c

    def rm(name, cols):
        start, rows = ROW_AT[name]
        return rmap[start : start + rows, 0:cols]

    own_rows = slice(HALO, HALO + ROWS)

    def strip(src, dst, i, target):
        return send(q.at[src], q.at[dst], halo_s.at[i], halo_r.at[i], target)

    loads["heat"].wait()
    q[EXT:DEEP, :] = jnp.zeros((DEEP - EXT, WIDE), F32)

    loads["rows"].wait()
    loads["res"].wait()
    own_h, own_l = split(q[own_rows, SIDE : SIDE + COLS])
    r3 = rm("r3", ROWS)
    by_rows_h, by_rows_l = split(mm_right(r3, own_h, own_l))
    top = mm_left(by_rows_h, by_rows_l, cres[...])
    at_right = lax.broadcasted_iota(jnp.int32, (32, 128), 1) < 64
    es[:, 0:128] = jnp.where(at_right, 0.0, top[:, 128:256])
    es[:, 128:256] = top[:, 0:128]
    es[:, 256:384] = jnp.where(at_right, top[:, 128:256], 0.0)
    row_part = {-1: slice(0, 8), 0: slice(8, 24), 1: slice(24, 32)}
    col_part = {-1: slice(0, 128), 0: slice(128, 256), 1: slice(256, 384)}
    pl.semaphore_wait(barrier, jnp.where((qi == 0) | (qi == NQ - 1), count + NQ, count))
    rims = []
    for i, (dw, dn) in enumerate(around):
        dst = nb.at[i] if dw else nb_mid.at[i // 4]
        rims.append(
            send(es.at[row_part[dw], col_part[dn]], dst, rim_s.at[i], rim_r.at[i], dev(dw, dn))
        )

    strips = [
        strip((own_rows, slice(COLS, COLS + SIDE)), (own_rows, slice(0, SIDE)), 0, dev(0, 1)),
        strip((own_rows, slice(SIDE, 2 * SIDE)), (own_rows, slice(SIDE + COLS, WIDE)), 1, dev(0, -1)),
    ]

    loads["top_rows"].wait()
    loads["sort"].wait()
    halves = [split(aw[:, 512 * p : 512 * (p + 1)]) for p in range(2)]
    sorted_cols = mm(
        jnp.concatenate([halves[0][0], halves[1][0], halves[0][1], halves[1][1]], axis=0), perm[...]
    )
    sorted_cols = sorted_cols[0:32] + sorted_cols[32:64]
    for p in range(2):
        for k in range(NQ):
            to[k, p] = sorted_cols[16 * p : 16 * (p + 1), 128 * k : 128 * (k + 1)]
    plane = [
        send(to.at[(qi + k) % NQ], ar.at[qi], aa_s.at[k - 1], aa_r.at[k - 1], in_row(k, 0))
        for k in (1, 2, 3)
    ]
    ar[qi] = to[qi]

    def rim_copy(src, dst, side, p, dz):
        return pltpu.make_async_remote_copy(
            src_ref=src, dst_ref=dst, send_sem=ah_s.at[p], recv_sem=ah_r.at[side],
            device_id=(((z + dz + NZ) % NZ) * NQ + p, n), device_id_type=MESH,
        )

    def rim_down(p):
        return rim_copy(to.at[p, :, 8:16], at, 0, p, 1)

    def rim_up(p):
        return rim_copy(to.at[p, :, 0:8], ab, 1, p, -1)

    @pl.when(qi == NQ - 1)
    def _():
        for p in range(NQ):
            rim_down(p).start()

    @pl.when(qi == 0)
    def _():
        for p in range(NQ):
            rim_up(p).start()

    loads["top_cols"].wait()
    sides = [
        send(bx.at[128:136], bx.at[0:8], bx_s.at[0], bx_r.at[0], dev(0, 1)),
        send(bx.at[8:16], bx.at[136:144], bx_s.at[1], bx_r.at[1], dev(0, -1)),
    ]
    for c in strips:
        c.wait_recv()
    outer = [
        strip(slice(ROWS, ROWS + HALO), slice(0, HALO), 2, dev(1, 0)),
        strip(slice(HALO, 2 * HALO), slice(HALO + ROWS, EXT), 3, dev(-1, 0)),
    ]

    for c in rims:
        c.wait_recv()
    mid = nb_mid[0] + nb_mid[1]
    halves = [
        (es[8 + 8 * p : 16 + 8 * p, 128:256] + mid[8 * p : 8 * p + 8])
        + (nb[first] + (nb[first + 1] + nb[first + 2]))
        for p, first in ((0, 5), (1, 0))
    ]
    g[z] = jnp.concatenate(halves, axis=0)

    column = [
        send(g.at[z], g.at[z], z_s.at[i], z_r.at[i], in_z(dz)) for i, dz in enumerate(along)
    ]

    loads["taps"].wait()

    low, high = jnp.where(w == 0, HALO, 0), jnp.where(w == NW - 1, HALO + ROWS, EXT)
    t0 = jnp.where(
        between((ROWS, DEEP), 1, low, high), band((ROWS, DEEP), 1, 8 - HALO, taps, 0), 0.0
    )

    def row_level(level, size, res, pro):
        th, tl = split(band((size, size), 1, 8, taps, level))
        tr_h, tr_l = split(mm_left(th, tl, res))
        return mm_right(pro, tr_h, tr_l)

    row_maps_of = (
        t0,
        row_level(1, 128, rm("r1", DEEP), rm("p1", 128)),
        row_level(2, 64, rm("r21", DEEP), rm("p12", 64)),
    )
    for i, m in enumerate(row_maps_of):
        hi, lo = split(m)
        at_i = slice(i * ROWS, (i + 1) * ROWS)
        mr[at_i, 0:DEEP] = hi
        mr[at_i, DEEP : 2 * DEEP] = lo
        mr[at_i, 2 * DEEP : 3 * DEEP] = hi

    fine_band = band((WIN, TILE), 0, 8 - MARGIN, taps, 0)
    coarse_bands = [split(band((size, size), 0, 8, taps, t)) for t, size in ((1, 128), (2, 64))]

    def col_maps_of(i, low, high):
        def cm(name, cols):
            start, rows = COL_AT[name]
            return cmap[i, start : start + rows, 0:cols]

        maps = [jnp.where(between((WIN, TILE), 0, low, high), fine_band, 0.0)]
        for (th, tl), res, pro in (
            (coarse_bands[0], cm("r1", 128), cm("p1", 128)),
            (coarse_bands[1], cm("r21", 64), cm("p12", 128)),
        ):
            tp_h, tp_l = split(mm_left(th, tl, pro))
            maps.append(mm_right(res, tp_h, tp_l))
        for t, m in enumerate(maps):
            hi, lo = split(m)
            cm_w[i, WIN * t : WIN * (t + 1), 0:TILE] = hi
            cm_w[i, WIN * t : WIN * (t + 1), TILE : 2 * TILE] = lo

    loads["cols"].wait()
    loads["rim_cols"].wait()
    col_maps_of(0, 0, WIN)
    col_maps_of(
        1,
        jnp.where(n == 0, MARGIN, 0),
        jnp.where(n == NN - 1, MARGIN + TILE, WIN),
    )

    for c in plane:
        c.wait_recv()
    for side, dst in ((0, at), (1, ab)):
        rim_copy(dst, dst, side, 0, 1).wait_recv()
    blocks = [at] + [ar.at[k] for k in range(NQ)] + [ab]
    a_h, a_l = split(
        jnp.concatenate(
            [jnp.concatenate([b[0], b[1]], axis=1) for b in blocks], axis=0
        )
    )
    for c in sides:
        c.wait_recv()

    @pl.loop(0, COLS // 128)
    def _(j):
        at_j = pl.ds(pl.multiple_of(128 * j, 128), 128)
        b_h[:, at_j], b_l[:, at_j] = split(bx[:, at_j])

    loads["top"].wait()

    for c in column:
        c.wait_recv()
    g_h, g_l = split(g[...].reshape(256, 128))
    ps[...] = mm_both(a_h, a_l, g_h, g_l)

    partial_sums = []
    for i, (k, dx) in enumerate(hops):
        start = pl.multiple_of(16 * ((qi + k) % NQ), 16)
        partial_sums.append(
            send(ps.at[pl.ds(start, 32)], pa.at[xl, k], pa_s.at[i], pa_r.at[i], in_row(k, dx))
        )
    own = pl.multiple_of(16 * qi, 16)
    pa[xl, 0] = ps[pl.ds(own, 32), :]

    for c in outer:
        c.wait_recv()

    @pl.loop(0, 5)
    def _(j):
        start = pl.multiple_of(128 * jnp.minimum(2 * j, SPAN // 128 - 2), 128)
        here = pltpu.roll(q[:, pl.ds(start, 384)], 384 - MARGIN, 1)[:, 0:256]
        hi, lo = split(here)
        res = mm(mr[...], jnp.concatenate([hi, hi, lo], axis=0))
        at_j = pl.ds(start, 256)
        y_hl[0, :, at_j], y_hl[1, :, at_j] = split(res)

    for c in partial_sums:
        c.wait_recv()
    for b in range(2):
        total = (pa[b, 0] + pa[b, 1]) + (pa[b, 2] + pa[b, 3])
        xb[y, :, 128 * b : 128 * (b + 1)] = total[7:31, :]
    lines = [
        send(xb.at[y], xb.at[y], xb_s.at[k - 1], xb_r.at[k - 1], in_y(k)) for k in range(1, NY)
    ]

    @pl.loop(0, TILES)
    def _(j):
        at_rim = ((j == 0) & (n == 0)) | ((j == TILES - 1) & (n == NN - 1))
        at_j = pl.ds(pl.multiple_of(TILE * j, TILE), WIN)
        windows = [
            jnp.concatenate([y_hl[p, t * ROWS : (t + 1) * ROWS, at_j] for t in range(3)], axis=1)
            for p in range(2)
        ]
        both = mm(jnp.concatenate(windows, axis=0), cm_w[jnp.where(at_rim, 1, 0)])
        acc[:, pl.ds(pl.multiple_of(TILE * j, TILE), TILE)] = both[0:ROWS, 0:TILE] + (
            both[0:ROWS, TILE:] + both[ROWS:, 0:TILE]
        )

    for c in lines:
        c.wait_recv()
    lines_in = jnp.concatenate([xb[i] for i in range(NY)], axis=1)
    x_h, x_l = split(jnp.concatenate([lines_in, jnp.zeros((8, COLS), F32)], axis=0))
    with_hi = mm_nt(jnp.concatenate([x_h, x_l], axis=0), b_h[...])
    e_h, e_l = split(with_hi[0:32] + (with_hi[32:64] + mm_nt(x_h, b_l[...])))
    f_h, f_l = split(mm_left(e_h, e_l, ctop[...]))
    ur = rm("top", 32)
    pieces = []
    for i in range(4):
        at_i = slice(256 * i, 256 * (i + 1))
        acc[:, at_i] += mm_right(ur, f_h[:, at_i], f_l[:, at_i])
        pieces.append(pltpu.make_async_copy(acc.at[:, at_i], out.at[:, at_i], out_s.at[i]))
        pieces[-1].start()

    for c in rims + strips + plane + sides + outer + column + partial_sums + lines:
        c.wait_send()

    @pl.when(qi == NQ - 1)
    def _():
        for p in range(NQ):
            rim_down(p).wait_send()

    @pl.when(qi == 0)
    def _():
        for p in range(NQ):
            rim_up(p).wait_send()

    for c in pieces:
        c.wait()


def shards(maps, heat_power, level_taps, top_rows, top_cols):
    far_memory = pl.BlockSpec(memory_space=pltpu.HBM)
    sems = [10, 8, 8, 4, 4, 3, 3, 4, 2, 2, 2, 15, 15, 7, 7, 3, 3, 4]
    words = lambda *shape: pltpu.VMEM(shape, F32)
    halves = lambda *shape: pltpu.VMEM(shape, BF16)
    return pl.pallas_call(
        kernel,
        out_shape=jax.ShapeDtypeStruct((ROWS, COLS), F32),
        in_specs=[far_memory] * (4 + len(maps)),
        out_specs=far_memory,
        scratch_shapes=[
            pltpu.SMEM((3, TAPS), F32),
            words(DEEP, WIDE),
            words(16, COLS),
            words(NQ, 2, 16, 128),
            words(NQ, 2, 16, 128),
            words(2, 8, 128),
            words(2, 8, 128),
            words(144, COLS),
            halves(*maps[0].shape[1:]),
            halves(2, *maps[1].shape[1:]),
            halves(*maps[2].shape[1:]),
            halves(*maps[3].shape[1:]),
            halves(*maps[4].shape),
            halves(3 * ROWS, 3 * DEEP),
            halves(2, 3 * ROWS, SPAN),
            halves(144, COLS),
            halves(144, COLS),
            halves(2, 3 * WIN, 2 * TILE),
            words(32, 384),
            words(8, 8, 128),
            words(2, 16, 128),
            words(NZ, 16, 128),
            words(80, 128),
            words(2, NQ, 32, 128),
            words(NY, 24, 256),
            words(ROWS, COLS),
        ]
        + [pltpu.SemaphoreType.DMA((k,)) for k in sems],
        compiler_params=pltpu.CompilerParams(
            collective_id=0, has_side_effects=True, vmem_limit_bytes=62 * 1024 * 1024
        ),
    )(heat_power, level_taps, top_rows, top_cols, *maps)


def solution(mesh):
    maps = constants()
    return jax.shard_map(
        functools.partial(shards, maps),
        mesh=mesh,
        in_specs=(P("wide", "narrow"), P(), P("wide", None), P("narrow", None)),
        out_specs=P("wide", "narrow"),
        check_vma=False,
    )
```

```python
import functools

import jax
import jax.numpy as jnp
import ml_dtypes
import numpy as np
from jax import lax
from jax.experimental import pallas as pl
from jax.experimental.pallas import tpu as pltpu
from jax.sharding import PartitionSpec as P

F32 = jnp.float32
BF16 = jnp.bfloat16
MESH = pl.DeviceIdType.MESH
TAPS = 17
NZ, NQ, NN, NY = 16, 4, 8, 4
NW = NZ * NQ
ROWS, COLS = 128, 1024
HALO = 40
EXT = ROWS + 2 * HALO
DEEP = 256
SIDE = 128
WIDE = COLS + 2 * SIDE
TILE = 128
MARGIN = 64
WIN = TILE + 2 * MARGIN
SPAN = COLS + 2 * MARGIN
TILES = COLS // TILE


def restriction(out_n, out_off, in_n, in_off, first, out_end, in_end):
    out_at = np.arange(out_n)[:, None] + out_off
    in_at = np.arange(in_n)[None, :] + in_off
    d = in_at - 2 * out_at
    m = np.where((d == 0) | (d == 1), 0.375, 0.0) + np.where((d == -1) | (d == 2), 0.125, 0.0)
    if first:
        m = np.where((out_at >= 0) & (in_at >= 0), m, 0.0)
    if out_end is not None:
        m = np.where((out_at < out_end) & (in_at < in_end), m, 0.0)
    return m


def prolongation(out_n, out_off, in_n, in_off, first, in_end):
    out_at = np.arange(out_n)[:, None] + out_off
    in_at = np.arange(in_n)[None, :] + in_off
    d = out_at - 2 * in_at
    m = np.where((d == 0) | (d == 1), 0.75, 0.0) + np.where((d == -1) | (d == 2), 0.25, 0.0)
    if first:
        m = np.where(in_at >= 0, m, 0.0)
    if in_end is not None:
        m = np.where(in_at < in_end, m, 0.0)
    return m


def level_maps(block, off, size, variant):
    first, last = variant == 0, variant == 2
    end = [block >> t if last else None for t in range(4)]
    r1 = restriction(size // 2, -off // 2, size, -off, first, end[1], end[0])
    r2 = restriction(size // 4, -off // 4, size // 2, -off // 2, first, end[2], end[1])
    p1 = prolongation(block, 0, size // 2, -off // 2, first, end[1])
    p2 = prolongation(size // 2, -off // 2, size // 4, -off // 4, first, end[2])
    return r1, r2, p1, p2


def top_prolong(block, in_n, in_off, variant):
    first, last = variant == 0, variant == 2
    end = [block >> t if last else None for t in range(4)]
    p3 = prolongation(block // 4 + 4, -2, in_n, in_off, first, end[3])
    p2 = prolongation(block // 2 + 4, -2, block // 4 + 4, -2, first, end[2])
    p1 = prolongation(block, 0, block // 2 + 4, -2, first, end[1])
    return p1 @ p2 @ p3


def own_to_top(block, variant):
    first, last = variant == 0, variant == 2
    end = [block >> t if last else None for t in range(4)]
    r1 = restriction(block // 2 + 16, -8, block, 0, first, end[1], end[0])
    r2 = restriction(block // 4 + 16, -8, block // 2 + 16, -8, first, end[2], end[1])
    r3 = restriction(block // 8 + 16, -8, block // 4 + 16, -8, first, end[3], end[2])
    return r3 @ r2 @ r1


def padded(m, rows, cols):
    out = np.zeros((rows, cols))
    out[: m.shape[0], : m.shape[1]] = m
    return out


ROW_AT = dict(r3=(0, 32), r1=(32, 128), r21=(160, 64), p1=(224, 128), p12=(352, 128), top=(480, 128))
COL_AT = dict(r1=(0, 256), r21=(256, 256), p1=(512, 128), p12=(640, 64))


def constants():
    row_maps, col_maps, col_top, col_res = [], [], [], []
    for v in range(3):
        r1, r2, p1, p2 = level_maps(ROWS, HALO, EXT, v)
        row_maps.append(
            np.concatenate(
                [
                    padded(own_to_top(ROWS, v), 32, 256),
                    padded(r1, 128, 256),
                    padded(r2 @ r1, 64, 256),
                    padded(p1, 128, 256),
                    padded(p1 @ p2, 128, 256),
                    padded(top_prolong(ROWS, 24, -1, v), 128, 256),
                ]
            )
        )
        r1, r2, p1, p2 = level_maps(TILE, MARGIN, WIN, v)
        col_maps.append(
            np.concatenate([r1.T, padded((r2 @ r1).T, 256, 128), p1.T, (p1 @ p2).T])
        )
        res = own_to_top(COLS, v)
        col_res.append(np.concatenate([res[8:136], res[136:144], np.zeros((112, COLS)), res[0:8]]).T)
        col_top.append(top_prolong(COLS, 144, -8, v).T)
    at = np.arange(512)
    sort = np.zeros((512, 512))
    sort[at, 128 * (at // 16 % 4) + 16 * (at // 64) + at % 16] = 1.0
    as_bf16 = lambda ms: np.stack(ms).astype(ml_dtypes.bfloat16)
    return as_bf16(row_maps), as_bf16(col_maps), as_bf16(col_res), as_bf16(col_top), as_bf16(sort)


def split(x):
    hi = x.astype(BF16)
    return hi, (x - hi.astype(F32)).astype(BF16)


def mm(a, b):
    return jnp.dot(a, b, preferred_element_type=F32)


def mm_right(a, b_h, b_l):
    return mm(jnp.concatenate([a, a], axis=1), jnp.concatenate([b_h, b_l], axis=0))


def mm_left(a_h, a_l, b):
    res = mm(jnp.concatenate([a_h, a_l], axis=0), b)
    return res[0 : a_h.shape[0]] + res[a_h.shape[0] :]


def mm_both(a_h, a_l, b_h, b_l):
    m, n = a_h.shape[0], b_h.shape[1]
    res = mm(jnp.concatenate([a_h, a_l], axis=0), jnp.concatenate([b_h, b_l], axis=1))
    return res[0:m, 0:n] + (res[0:m, n:] + res[m:, 0:n])


def mm_nt(a, b):
    return lax.dot_general(a, b, (((1,), (1,)), ((), ())), preferred_element_type=F32)


def band(shape, in_dim, shift, taps, level):
    row = lax.broadcasted_iota(jnp.int32, (8, 256), 0)
    col = lax.broadcasted_iota(jnp.int32, (8, 256), 1)
    d = ((row - col if in_dim == 0 else col - row) + shift + 512) & 255
    first = jnp.zeros((8, 256), F32)
    for k in range(TAPS):
        first = jnp.where(d == k, taps[level, k], first)
    parts = [first] + [pltpu.roll(first, at, 1) for at in range(8, shape[0], 8)]
    return jnp.concatenate([p[:, 0 : shape[1]] for p in parts], axis=0)


def between(shape, dim, low, high):
    at = lax.broadcasted_iota(jnp.int32, shape, dim)
    return (at >= low) & (at < high)


def kernel(
    heat, taps_in, top_rows, top_cols, row_maps, col_maps, col_res, col_top, sort, out,
    taps, q, aw, to, ar, at, ab, bx, rmap, cmap, cres, ctop, perm,
    mr, y_hl, b_h, b_l, cm_w, es, nb, nb_mid, g, ps, pa, xb, acc,
    load_sem, rim_s, rim_r, halo_s, halo_r, aa_s, aa_r, ah_s, ah_r, bx_s, bx_r,
    z_s, z_r, pa_s, pa_r, xb_s, xb_r, out_s,
):
    w, n = lax.axis_index("wide"), lax.axis_index("narrow")
    z, qi = w // NQ, w % NQ
    y, xl = n // 2, n % 2

    def dev(dw, dn):
        return ((w + dw + NW) % NW, (n + dn + NN) % NN)

    def in_z(dz):
        return (((z + dz + NZ) % NZ) * NQ + qi, n)

    def in_row(k, dx):
        return (z * NQ + (qi + k + NQ) % NQ, 2 * y + (xl + dx) % 2)

    def in_y(dy):
        return (w, 2 * ((y + dy + NY) % NY) + xl)

    row_v = jnp.where(w == 0, 0, jnp.where(w == NW - 1, 2, 1))
    col_v = jnp.where(n == 0, 0, jnp.where(n == NN - 1, 2, 1))

    pairs = dict(
        heat=(heat, q.at[HALO : HALO + ROWS, SIDE : SIDE + COLS]),
        rows=(row_maps.at[row_v], rmap),
        res=(col_res.at[col_v], cres),
        top_rows=(top_rows, aw),
        sort=(sort, perm),
        top_cols=(top_cols, bx.at[8:136]),
        taps=(taps_in, taps),
        cols=(col_maps.at[1], cmap.at[0]),
        rim_cols=(col_maps.at[col_v], cmap.at[1]),
        top=(col_top.at[col_v], ctop),
    )
    loads = {
        name: pltpu.make_async_copy(src, dst, load_sem.at[i])
        for i, (name, (src, dst)) in enumerate(pairs.items())
    }
    for name in ("heat", "rows", "res"):
        loads[name].start()

    barrier = pltpu.get_barrier_semaphore()
    around = [(dw, dn) for dw in (-1, 0, 1) for dn in (-1, 0, 1) if (dw, dn) != (0, 0)]
    greet = [dev(dw, dn) for dw, dn in around]
    hops = [(k, dx) for k in range(NQ) for dx in range(2) if (k, dx) != (0, 0)]
    greet += [in_row(-k, dx) for k, dx in hops]
    greet += [in_y(dy) for dy in (1, 2, 3)]
    along = [8] + [d for dz in range(7, 0, -1) for d in (dz, -dz)]
    greet += [in_z(dz) for dz in along]
    count = len(greet)
    greet += [(((z + NZ - 1) % NZ) * NQ + NQ - 1, n), (((z + 1) % NZ) * NQ, n)]
    for target in greet:
        pl.semaphore_signal(barrier, inc=1, device_id=target, device_id_type=MESH)
    for name in ("top_rows", "sort", "top_cols", "taps", "cols", "rim_cols", "top"):
        loads[name].start()

    def send(src, dst, send_sem, recv_sem, target):
        c = pltpu.make_async_remote_copy(
            src_ref=src, dst_ref=dst, send_sem=send_sem, recv_sem=recv_sem,
            device_id=target, device_id_type=MESH,
        )
        c.start()
        return c

    def rm(name, cols):
        start, rows = ROW_AT[name]
        return rmap[start : start + rows, 0:cols]

    own_rows = slice(HALO, HALO + ROWS)

    def strip(src, dst, i, target):
        return send(q.at[src], q.at[dst], halo_s.at[i], halo_r.at[i], target)

    loads["heat"].wait()
    q[EXT:DEEP, :] = jnp.zeros((DEEP - EXT, WIDE), F32)

    loads["rows"].wait()
    loads["res"].wait()
    own_h, own_l = split(q[own_rows, SIDE : SIDE + COLS])
    r3 = rm("r3", ROWS)
    by_rows_h, by_rows_l = split(mm_right(r3, own_h, own_l))
    top = mm_left(by_rows_h, by_rows_l, cres[...])
    at_right = lax.broadcasted_iota(jnp.int32, (32, 128), 1) < 64
    es[:, 0:128] = jnp.where(at_right, 0.0, top[:, 128:256])
    es[:, 128:256] = top[:, 0:128]
    es[:, 256:384] = jnp.where(at_right, top[:, 128:256], 0.0)
    row_part = {-1: slice(0, 8), 0: slice(8, 24), 1: slice(24, 32)}
    col_part = {-1: slice(0, 128), 0: slice(128, 256), 1: slice(256, 384)}
    pl.semaphore_wait(barrier, jnp.where((qi == 0) | (qi == NQ - 1), count + NQ, count))
    rims = []
    for i, (dw, dn) in enumerate(around):
        dst = nb.at[i] if dw else nb_mid.at[i // 4]
        rims.append(
            send(es.at[row_part[dw], col_part[dn]], dst, rim_s.at[i], rim_r.at[i], dev(dw, dn))
        )

    loads["top_rows"].wait()
    loads["sort"].wait()
    halves = [split(aw[:, 512 * p : 512 * (p + 1)]) for p in range(2)]
    sorted_cols = mm(
        jnp.concatenate([halves[0][0], halves[1][0], halves[0][1], halves[1][1]], axis=0), perm[...]
    )
    sorted_cols = sorted_cols[0:32] + sorted_cols[32:64]
    for p in range(2):
        for k in range(NQ):
            to[k, p] = sorted_cols[16 * p : 16 * (p + 1), 128 * k : 128 * (k + 1)]
    plane = [
        send(to.at[(qi + k) % NQ], ar.at[qi], aa_s.at[k - 1], aa_r.at[k - 1], in_row(k, 0))
        for k in (1, 2, 3)
    ]
    ar[qi] = to[qi]

    def rim_copy(src, dst, side, p, dz):
        return pltpu.make_async_remote_copy(
            src_ref=src, dst_ref=dst, send_sem=ah_s.at[p], recv_sem=ah_r.at[side],
            device_id=(((z + dz + NZ) % NZ) * NQ + p, n), device_id_type=MESH,
        )

    def rim_down(p):
        return rim_copy(to.at[p, :, 8:16], at, 0, p, 1)

    def rim_up(p):
        return rim_copy(to.at[p, :, 0:8], ab, 1, p, -1)

    @pl.when(qi == NQ - 1)
    def _():
        for p in range(NQ):
            rim_down(p).start()

    @pl.when(qi == 0)
    def _():
        for p in range(NQ):
            rim_up(p).start()

    for c in rims:
        c.wait_recv()
    mid = nb_mid[0] + nb_mid[1]
    halves = [
        (es[8 + 8 * p : 16 + 8 * p, 128:256] + mid[8 * p : 8 * p + 8])
        + (nb[first] + (nb[first + 1] + nb[first + 2]))
        for p, first in ((0, 5), (1, 0))
    ]
    g[z] = jnp.concatenate(halves, axis=0)

    column = [
        send(g.at[z], g.at[z], z_s.at[i], z_r.at[i], in_z(dz)) for i, dz in enumerate(along)
    ]

    strips = [
        strip((own_rows, slice(COLS, COLS + SIDE)), (own_rows, slice(0, SIDE)), 0, dev(0, 1)),
        strip((own_rows, slice(SIDE, 2 * SIDE)), (own_rows, slice(SIDE + COLS, WIDE)), 1, dev(0, -1)),
    ]
    loads["top_cols"].wait()
    sides = [
        send(bx.at[128:136], bx.at[0:8], bx_s.at[0], bx_r.at[0], dev(0, 1)),
        send(bx.at[8:16], bx.at[136:144], bx_s.at[1], bx_r.at[1], dev(0, -1)),
    ]

    loads["taps"].wait()

    low, high = jnp.where(w == 0, HALO, 0), jnp.where(w == NW - 1, HALO + ROWS, EXT)
    t0 = jnp.where(
        between((ROWS, DEEP), 1, low, high), band((ROWS, DEEP), 1, 8 - HALO, taps, 0), 0.0
    )

    def row_level(level, size, res, pro):
        th, tl = split(band((size, size), 1, 8, taps, level))
        tr_h, tr_l = split(mm_left(th, tl, res))
        return mm_right(pro, tr_h, tr_l)

    row_maps_of = (
        t0,
        row_level(1, 128, rm("r1", DEEP), rm("p1", 128)),
        row_level(2, 64, rm("r21", DEEP), rm("p12", 64)),
    )
    for i, m in enumerate(row_maps_of):
        hi, lo = split(m)
        at_i = slice(i * ROWS, (i + 1) * ROWS)
        mr[at_i, 0:DEEP] = hi
        mr[at_i, DEEP : 2 * DEEP] = lo
        mr[at_i, 2 * DEEP : 3 * DEEP] = hi

    for c in strips:
        c.wait_recv()
    outer = [
        strip(slice(ROWS, ROWS + HALO), slice(0, HALO), 2, dev(1, 0)),
        strip(slice(HALO, 2 * HALO), slice(HALO + ROWS, EXT), 3, dev(-1, 0)),
    ]

    fine_band = band((WIN, TILE), 0, 8 - MARGIN, taps, 0)
    coarse_bands = [split(band((size, size), 0, 8, taps, t)) for t, size in ((1, 128), (2, 64))]

    def col_maps_of(i, low, high):
        def cm(name, cols):
            start, rows = COL_AT[name]
            return cmap[i, start : start + rows, 0:cols]

        maps = [jnp.where(between((WIN, TILE), 0, low, high), fine_band, 0.0)]
        for (th, tl), res, pro in (
            (coarse_bands[0], cm("r1", 128), cm("p1", 128)),
            (coarse_bands[1], cm("r21", 64), cm("p12", 128)),
        ):
            tp_h, tp_l = split(mm_left(th, tl, pro))
            maps.append(mm_right(res, tp_h, tp_l))
        for t, m in enumerate(maps):
            hi, lo = split(m)
            cm_w[i, WIN * t : WIN * (t + 1), 0:TILE] = hi
            cm_w[i, WIN * t : WIN * (t + 1), TILE : 2 * TILE] = lo

    loads["cols"].wait()
    loads["rim_cols"].wait()
    col_maps_of(0, 0, WIN)
    col_maps_of(
        1,
        jnp.where(n == 0, MARGIN, 0),
        jnp.where(n == NN - 1, MARGIN + TILE, WIN),
    )

    for c in plane:
        c.wait_recv()
    for side, dst in ((0, at), (1, ab)):
        rim_copy(dst, dst, side, 0, 1).wait_recv()
    blocks = [at] + [ar.at[k] for k in range(NQ)] + [ab]
    plane_rows = jnp.concatenate(
        [jnp.concatenate([b[0], b[1]], axis=1) for b in blocks], axis=0
    )
    a_h, a_l = split(
        jnp.concatenate([plane_rows[16 * k + 7 : 16 * k + 31] for k in range(NQ)], axis=0)
    )
    for c in sides:
        c.wait_recv()

    @pl.loop(0, COLS // 128)
    def _(j):
        at_j = pl.ds(pl.multiple_of(128 * j, 128), 128)
        b_h[:, at_j], b_l[:, at_j] = split(bx[:, at_j])

    loads["top"].wait()

    for c in column:
        c.wait_recv()
    g_h, g_l = split(g[...].reshape(256, 128))
    ps[...] = mm_both(a_h, a_l, g_h, g_l).reshape(NQ, 24, 128)

    partial_sums = []
    for i, (k, dx) in enumerate(hops):
        partial_sums.append(
            send(ps.at[(qi + k) % NQ], pa.at[xl, k], pa_s.at[i], pa_r.at[i], in_row(k, dx))
        )
    pa[xl, 0] = ps[qi]

    for c in outer:
        c.wait_recv()

    @pl.loop(0, 5)
    def _(j):
        start = pl.multiple_of(128 * jnp.minimum(2 * j, SPAN // 128 - 2), 128)
        here = pltpu.roll(q[:, pl.ds(start, 384)], 384 - MARGIN, 1)[:, 0:256]
        hi, lo = split(here)
        res = mm(mr[...], jnp.concatenate([hi, hi, lo], axis=0))
        at_j = pl.ds(start, 256)
        y_hl[0, :, at_j], y_hl[1, :, at_j] = split(res)

    for c in partial_sums:
        c.wait_recv()
    for b in range(2):
        total = (pa[b, 0] + pa[b, 1]) + (pa[b, 2] + pa[b, 3])
        xb[y, :, 128 * b : 128 * (b + 1)] = total
    lines = [
        send(xb.at[y], xb.at[y], xb_s.at[k - 1], xb_r.at[k - 1], in_y(k)) for k in range(1, NY)
    ]

    @pl.loop(0, TILES)
    def _(j):
        at_rim = ((j == 0) & (n == 0)) | ((j == TILES - 1) & (n == NN - 1))
        at_j = pl.ds(pl.multiple_of(TILE * j, TILE), WIN)
        windows = [
            jnp.concatenate([y_hl[p, t * ROWS : (t + 1) * ROWS, at_j] for t in range(3)], axis=1)
            for p in range(2)
        ]
        both = mm(jnp.concatenate(windows, axis=0), cm_w[jnp.where(at_rim, 1, 0)])
        acc[:, pl.ds(pl.multiple_of(TILE * j, TILE), TILE)] = both[0:ROWS, 0:TILE] + (
            both[0:ROWS, TILE:] + both[ROWS:, 0:TILE]
        )

    for c in lines:
        c.wait_recv()
    lines_in = jnp.concatenate([xb[i] for i in range(NY)], axis=1)
    x_h, x_l = split(jnp.concatenate([lines_in, jnp.zeros((8, COLS), F32)], axis=0))
    with_hi = mm_nt(jnp.concatenate([x_h, x_l], axis=0), b_h[...])
    e_h, e_l = split(with_hi[0:32] + (with_hi[32:64] + mm_nt(x_h, b_l[...])))
    f_h, f_l = split(mm_left(e_h, e_l, ctop[...]))
    ur = rm("top", 32)
    pieces = []
    for i in range(4):
        at_i = slice(256 * i, 256 * (i + 1))
        acc[:, at_i] += mm_right(ur, f_h[:, at_i], f_l[:, at_i])
        pieces.append(pltpu.make_async_copy(acc.at[:, at_i], out.at[:, at_i], out_s.at[i]))
        pieces[-1].start()

    for c in rims + strips + plane + sides + outer + column + partial_sums + lines:
        c.wait_send()

    @pl.when(qi == NQ - 1)
    def _():
        for p in range(NQ):
            rim_down(p).wait_send()

    @pl.when(qi == 0)
    def _():
        for p in range(NQ):
            rim_up(p).wait_send()

    for c in pieces:
        c.wait()


def shards(maps, heat_power, level_taps, top_rows, top_cols):
    far_memory = pl.BlockSpec(memory_space=pltpu.HBM)
    sems = [10, 8, 8, 4, 4, 3, 3, 4, 2, 2, 2, 15, 15, 7, 7, 3, 3, 4]
    words = lambda *shape: pltpu.VMEM(shape, F32)
    halves = lambda *shape: pltpu.VMEM(shape, BF16)
    return pl.pallas_call(
        kernel,
        out_shape=jax.ShapeDtypeStruct((ROWS, COLS), F32),
        in_specs=[far_memory] * (4 + len(maps)),
        out_specs=far_memory,
        scratch_shapes=[
            pltpu.SMEM((3, TAPS), F32),
            words(DEEP, WIDE),
            words(16, COLS),
            words(NQ, 2, 16, 128),
            words(NQ, 2, 16, 128),
            words(2, 8, 128),
            words(2, 8, 128),
            words(144, COLS),
            halves(*maps[0].shape[1:]),
            halves(2, *maps[1].shape[1:]),
            halves(*maps[2].shape[1:]),
            halves(*maps[3].shape[1:]),
            halves(*maps[4].shape),
            halves(3 * ROWS, 3 * DEEP),
            halves(2, 3 * ROWS, SPAN),
            halves(144, COLS),
            halves(144, COLS),
            halves(2, 3 * WIN, 2 * TILE),
            words(32, 384),
            words(8, 8, 128),
            words(2, 16, 128),
            words(NZ, 16, 128),
            words(NQ, 24, 128),
            words(2, NQ, 24, 128),
            words(NY, 24, 256),
            words(ROWS, COLS),
        ]
        + [pltpu.SemaphoreType.DMA((k,)) for k in sems],
        compiler_params=pltpu.CompilerParams(
            collective_id=0, has_side_effects=True, vmem_limit_bytes=62 * 1024 * 1024
        ),
    )(heat_power, level_taps, top_rows, top_cols, *maps)


def solution(mesh):
    maps = constants()
    return jax.shard_map(
        functools.partial(shards, maps),
        mesh=mesh,
        in_specs=(P("wide", "narrow"), P(), P("wide", None), P("narrow", None)),
        out_specs=P("wide", "narrow"),
        check_vma=False,
    )
```

```python
import functools

import jax
import jax.numpy as jnp
import ml_dtypes
import numpy as np
from jax import lax
from jax.experimental import pallas as pl
from jax.experimental.pallas import tpu as pltpu
from jax.sharding import PartitionSpec as P

F32 = jnp.float32
BF16 = jnp.bfloat16
MESH = pl.DeviceIdType.MESH
TAPS = 17
NZ, NQ, NN, NY = 16, 4, 8, 4
NW = NZ * NQ
ROWS, COLS = 128, 1024
HALO = 40
EXT = ROWS + 2 * HALO
DEEP = 256
SIDE = 128
WIDE = COLS + 2 * SIDE
TILE = 128
MARGIN = 64
WIN = TILE + 2 * MARGIN
SPAN = COLS + 2 * MARGIN
TILES = COLS // TILE


def restriction(out_n, out_off, in_n, in_off, first, out_end, in_end):
    out_at = np.arange(out_n)[:, None] + out_off
    in_at = np.arange(in_n)[None, :] + in_off
    d = in_at - 2 * out_at
    m = np.where((d == 0) | (d == 1), 0.375, 0.0) + np.where((d == -1) | (d == 2), 0.125, 0.0)
    if first:
        m = np.where((out_at >= 0) & (in_at >= 0), m, 0.0)
    if out_end is not None:
        m = np.where((out_at < out_end) & (in_at < in_end), m, 0.0)
    return m


def prolongation(out_n, out_off, in_n, in_off, first, in_end):
    out_at = np.arange(out_n)[:, None] + out_off
    in_at = np.arange(in_n)[None, :] + in_off
    d = out_at - 2 * in_at
    m = np.where((d == 0) | (d == 1), 0.75, 0.0) + np.where((d == -1) | (d == 2), 0.25, 0.0)
    if first:
        m = np.where(in_at >= 0, m, 0.0)
    if in_end is not None:
        m = np.where(in_at < in_end, m, 0.0)
    return m


def level_maps(block, off, size, variant):
    first, last = variant == 0, variant == 2
    end = [block >> t if last else None for t in range(4)]
    r1 = restriction(size // 2, -off // 2, size, -off, first, end[1], end[0])
    r2 = restriction(size // 4, -off // 4, size // 2, -off // 2, first, end[2], end[1])
    p1 = prolongation(block, 0, size // 2, -off // 2, first, end[1])
    p2 = prolongation(size // 2, -off // 2, size // 4, -off // 4, first, end[2])
    return r1, r2, p1, p2


def top_prolong(block, in_n, in_off, variant):
    first, last = variant == 0, variant == 2
    end = [block >> t if last else None for t in range(4)]
    p3 = prolongation(block // 4 + 4, -2, in_n, in_off, first, end[3])
    p2 = prolongation(block // 2 + 4, -2, block // 4 + 4, -2, first, end[2])
    p1 = prolongation(block, 0, block // 2 + 4, -2, first, end[1])
    return p1 @ p2 @ p3


def own_to_top(block, variant):
    first, last = variant == 0, variant == 2
    end = [block >> t if last else None for t in range(4)]
    r1 = restriction(block // 2 + 16, -8, block, 0, first, end[1], end[0])
    r2 = restriction(block // 4 + 16, -8, block // 2 + 16, -8, first, end[2], end[1])
    r3 = restriction(block // 8 + 16, -8, block // 4 + 16, -8, first, end[3], end[2])
    return r3 @ r2 @ r1


def padded(m, rows, cols):
    out = np.zeros((rows, cols))
    out[: m.shape[0], : m.shape[1]] = m
    return out


ROW_AT = dict(r3=(0, 32), r1=(32, 128), r21=(160, 64), p1=(224, 128), p12=(352, 128), top=(480, 128))
COL_AT = dict(r1=(0, 256), r21=(256, 256), p1=(512, 128), p12=(640, 64))


def constants():
    row_maps, col_maps, col_top, col_res = [], [], [], []
    for v in range(3):
        r1, r2, p1, p2 = level_maps(ROWS, HALO, EXT, v)
        row_maps.append(
            np.concatenate(
                [
                    padded(own_to_top(ROWS, v), 32, 256),
                    padded(r1, 128, 256),
                    padded(r2 @ r1, 64, 256),
                    padded(p1, 128, 256),
                    padded(p1 @ p2, 128, 256),
                    padded(top_prolong(ROWS, 24, -1, v), 128, 256),
                ]
            )
        )
        r1, r2, p1, p2 = level_maps(TILE, MARGIN, WIN, v)
        col_maps.append(
            np.concatenate([r1.T, padded((r2 @ r1).T, 256, 128), p1.T, (p1 @ p2).T])
        )
        res = own_to_top(COLS, v)
        col_res.append(np.concatenate([res[8:136], res[136:144], np.zeros((112, COLS)), res[0:8]]).T)
        col_top.append(top_prolong(COLS, 144, -8, v).T)
    at = np.arange(512)
    sort = np.zeros((512, 512))
    sort[at, 128 * (at // 16 % 4) + 16 * (at // 64) + at % 16] = 1.0
    as_bf16 = lambda ms: np.stack(ms).astype(ml_dtypes.bfloat16)
    return as_bf16(row_maps), as_bf16(col_maps), as_bf16(col_res), as_bf16(col_top), as_bf16(sort)


def split(x):
    hi = x.astype(BF16)
    return hi, (x - hi.astype(F32)).astype(BF16)


def mm(a, b):
    return jnp.dot(a, b, preferred_element_type=F32)


def mm_right(a, b_h, b_l):
    return mm(jnp.concatenate([a, a], axis=1), jnp.concatenate([b_h, b_l], axis=0))


def mm_left(a_h, a_l, b):
    res = mm(jnp.concatenate([a_h, a_l], axis=0), b)
    return res[0 : a_h.shape[0]] + res[a_h.shape[0] :]


def mm_both(a_h, a_l, b_h, b_l):
    m, n = a_h.shape[0], b_h.shape[1]
    res = mm(jnp.concatenate([a_h, a_l], axis=0), jnp.concatenate([b_h, b_l], axis=1))
    return res[0:m, 0:n] + (res[0:m, n:] + res[m:, 0:n])


def mm_nt(a, b):
    return lax.dot_general(a, b, (((1,), (1,)), ((), ())), preferred_element_type=F32)


def band(shape, in_dim, shift, taps, level):
    row = lax.broadcasted_iota(jnp.int32, (8, 256), 0)
    col = lax.broadcasted_iota(jnp.int32, (8, 256), 1)
    d = ((row - col if in_dim == 0 else col - row) + shift + 512) & 255
    first = jnp.zeros((8, 256), F32)
    for k in range(TAPS):
        first = jnp.where(d == k, taps[level, k], first)
    parts = [first] + [pltpu.roll(first, at, 1) for at in range(8, shape[0], 8)]
    return jnp.concatenate([p[:, 0 : shape[1]] for p in parts], axis=0)


def between(shape, dim, low, high):
    at = lax.broadcasted_iota(jnp.int32, shape, dim)
    return (at >= low) & (at < high)


def kernel(
    heat, taps_in, top_rows, top_cols, row_maps, col_maps, col_res, col_top, sort, near_out, top_out, row_out,
    taps, q, aw, to, ar, at, ab, bx, rmap, cmap, cres, ctop, perm,
    mr, y_hl, b_h, b_l, cm_w, es, nb, nb_mid, g, ps, pa, xb, acc, top_f, top_u,
    load_sem, rim_s, rim_r, halo_s, halo_r, aa_s, aa_r, ah_s, ah_r, bx_s, bx_r,
    z_s, z_r, pa_s, pa_r, xb_s, xb_r, out_s,
):
    w, n = lax.axis_index("wide"), lax.axis_index("narrow")
    rem = lax.rem
    z, qi = lax.div(w, NQ), rem(w, NQ)
    y, xl = lax.div(n, 2), rem(n, 2)
    row_at = z * NQ
    pair_at = n - xl

    def dev(dw, dn):
        return (rem(w + (dw + NW), NW) if dw else w, rem(n + (dn + NN), NN) if dn else n)

    def in_z(dz):
        return (rem(w + (dz + NZ) * NQ, NW), n)

    def in_row(k, dx):
        return (row_at + rem(qi + (k + NQ), NQ) if k else w, pair_at + 1 - xl if dx else n)

    def in_y(dy):
        return (w, rem(n + 2 * dy, NN))

    row_v = jnp.where(w == 0, 0, jnp.where(w == NW - 1, 2, 1))
    col_v = jnp.where(n == 0, 0, jnp.where(n == NN - 1, 2, 1))

    pairs = dict(
        heat=(heat, q.at[HALO : HALO + ROWS, SIDE : SIDE + COLS]),
        rows=(row_maps.at[row_v], rmap),
        res=(col_res.at[col_v], cres),
        top_rows=(top_rows, aw),
        sort=(sort, perm),
        top_cols=(top_cols, bx.at[8:136]),
        taps=(taps_in, taps),
        cols=(col_maps.at[1], cmap.at[0]),
        rim_cols=(col_maps.at[col_v], cmap.at[1]),
        top=(col_top.at[col_v], ctop),
    )
    loads = {
        name: pltpu.make_async_copy(src, dst, load_sem.at[i])
        for i, (name, (src, dst)) in enumerate(pairs.items())
    }
    for name in ("heat", "rows", "res"):
        loads[name].start()

    barrier = pltpu.get_barrier_semaphore()
    around = [(dw, dn) for dw in (-1, 0, 1) for dn in (-1, 0, 1) if (dw, dn) != (0, 0)]
    greet = [dev(dw, dn) for dw, dn in around]
    hops = [(k, dx) for k in range(NQ) for dx in range(2) if (k, dx) != (0, 0)]
    greet += [in_row(-k, dx) for k, dx in hops]
    greet += [in_y(dy) for dy in (1, 2, 3)]
    along = [8] + [d for dz in range(7, 0, -1) for d in (dz, -dz)]
    greet += [in_z(dz) for dz in along]
    count = len(greet)
    greet += [(rem(row_at + (NW - 1), NW), n), (rem(row_at + NQ, NW), n)]
    for target in greet:
        pl.semaphore_signal(barrier, inc=1, device_id=target, device_id_type=MESH)
    for name in ("top_rows", "sort", "top_cols", "taps", "cols", "rim_cols", "top"):
        loads[name].start()

    def send(src, dst, send_sem, recv_sem, target):
        c = pltpu.make_async_remote_copy(
            src_ref=src, dst_ref=dst, send_sem=send_sem, recv_sem=recv_sem,
            device_id=target, device_id_type=MESH,
        )
        c.start()
        return c

    def rm(name, cols):
        start, rows = ROW_AT[name]
        return rmap[start : start + rows, 0:cols]

    own_rows = slice(HALO, HALO + ROWS)

    def strip(src, dst, i, target):
        return send(q.at[src], q.at[dst], halo_s.at[i], halo_r.at[i], target)

    loads["heat"].wait()
    q[EXT:DEEP, :] = jnp.zeros((DEEP - EXT, WIDE), F32)

    loads["rows"].wait()
    loads["res"].wait()
    own_h, own_l = split(q[own_rows, SIDE : SIDE + COLS])
    r3 = rm("r3", ROWS)
    by_rows_h, by_rows_l = split(mm_right(r3, own_h, own_l))
    top = mm_left(by_rows_h, by_rows_l, cres[...])
    at_right = lax.broadcasted_iota(jnp.int32, (32, 128), 1) < 64
    es[:, 0:128] = jnp.where(at_right, 0.0, top[:, 128:256])
    es[:, 128:256] = top[:, 0:128]
    es[:, 256:384] = jnp.where(at_right, top[:, 128:256], 0.0)
    row_part = {-1: slice(0, 8), 0: slice(8, 24), 1: slice(24, 32)}
    col_part = {-1: slice(0, 128), 0: slice(128, 256), 1: slice(256, 384)}
    pl.semaphore_wait(barrier, jnp.where((qi == 0) | (qi == NQ - 1), count + NQ, count))
    rims = []
    for i, (dw, dn) in enumerate(around):
        dst = nb.at[i] if dw else nb_mid.at[i // 4]
        rims.append(
            send(es.at[row_part[dw], col_part[dn]], dst, rim_s.at[i], rim_r.at[i], dev(dw, dn))
        )

    strips = [
        strip((own_rows, slice(COLS, COLS + SIDE)), (own_rows, slice(0, SIDE)), 0, dev(0, 1)),
        strip((own_rows, slice(SIDE, 2 * SIDE)), (own_rows, slice(SIDE + COLS, WIDE)), 1, dev(0, -1)),
    ]

    loads["top_rows"].wait()
    loads["sort"].wait()
    halves = [split(aw[:, 512 * p : 512 * (p + 1)]) for p in range(2)]
    sorted_cols = mm(
        jnp.concatenate([halves[0][0], halves[1][0], halves[0][1], halves[1][1]], axis=0), perm[...]
    )
    sorted_cols = sorted_cols[0:32] + sorted_cols[32:64]
    for p in range(2):
        for k in range(NQ):
            to[k, p] = sorted_cols[16 * p : 16 * (p + 1), 128 * k : 128 * (k + 1)]
    plane = [
        send(to.at[rem(qi + k, NQ)], ar.at[qi], aa_s.at[k - 1], aa_r.at[k - 1], in_row(k, 0))
        for k in (1, 2, 3)
    ]
    ar[qi] = to[qi]

    def rim_copy(src, dst, side, p, dz):
        return pltpu.make_async_remote_copy(
            src_ref=src, dst_ref=dst, send_sem=ah_s.at[p], recv_sem=ah_r.at[side],
            device_id=(rem(row_at + ((dz + NZ) * NQ + p), NW), n), device_id_type=MESH,
        )

    def rim_down(p):
        return rim_copy(to.at[p, :, 8:16], at, 0, p, 1)

    def rim_up(p):
        return rim_copy(to.at[p, :, 0:8], ab, 1, p, -1)

    @pl.when(qi == NQ - 1)
    def _():
        for p in range(NQ):
            rim_down(p).start()

    @pl.when(qi == 0)
    def _():
        for p in range(NQ):
            rim_up(p).start()

    for c in rims:
        c.wait_recv()
    mid = nb_mid[0] + nb_mid[1]
    halves = [
        (es[8 + 8 * p : 16 + 8 * p, 128:256] + mid[8 * p : 8 * p + 8])
        + (nb[first] + (nb[first + 1] + nb[first + 2]))
        for p, first in ((0, 5), (1, 0))
    ]
    g[z] = jnp.concatenate(halves, axis=0)

    column = [
        send(g.at[z], g.at[z], z_s.at[i], z_r.at[i], in_z(dz)) for i, dz in enumerate(along)
    ]

    for c in strips:
        c.wait_recv()
    outer = [
        strip(slice(ROWS, ROWS + HALO), slice(0, HALO), 2, dev(1, 0)),
        strip(slice(HALO, 2 * HALO), slice(HALO + ROWS, EXT), 3, dev(-1, 0)),
    ]

    loads["top_cols"].wait()
    sides = [
        send(bx.at[128:136], bx.at[0:8], bx_s.at[0], bx_r.at[0], dev(0, 1)),
        send(bx.at[8:16], bx.at[136:144], bx_s.at[1], bx_r.at[1], dev(0, -1)),
    ]

    loads["taps"].wait()

    low, high = jnp.where(w == 0, HALO, 0), jnp.where(w == NW - 1, HALO + ROWS, EXT)
    t0 = jnp.where(
        between((ROWS, DEEP), 1, low, high), band((ROWS, DEEP), 1, 8 - HALO, taps, 0), 0.0
    )

    def row_level(level, size, res, pro):
        th, tl = split(band((size, size), 1, 8, taps, level))
        tr_h, tr_l = split(mm_left(th, tl, res))
        return mm_right(pro, tr_h, tr_l)

    row_maps_of = (
        t0,
        row_level(1, 128, rm("r1", DEEP), rm("p1", 128)),
        row_level(2, 64, rm("r21", DEEP), rm("p12", 64)),
    )
    for i, m in enumerate(row_maps_of):
        hi, lo = split(m)
        at_i = slice(i * ROWS, (i + 1) * ROWS)
        mr[at_i, 0:DEEP] = hi
        mr[at_i, DEEP : 2 * DEEP] = lo
        mr[at_i, 2 * DEEP : 3 * DEEP] = hi

    fine_band = band((WIN, TILE), 0, 8 - MARGIN, taps, 0)
    coarse_bands = [split(band((size, size), 0, 8, taps, t)) for t, size in ((1, 128), (2, 64))]

    def col_maps_of(i, low, high):
        def cm(name, cols):
            start, rows = COL_AT[name]
            return cmap[i, start : start + rows, 0:cols]

        maps = [jnp.where(between((WIN, TILE), 0, low, high), fine_band, 0.0)]
        for (th, tl), res, pro in (
            (coarse_bands[0], cm("r1", 128), cm("p1", 128)),
            (coarse_bands[1], cm("r21", 64), cm("p12", 128)),
        ):
            tp_h, tp_l = split(mm_left(th, tl, pro))
            maps.append(mm_right(res, tp_h, tp_l))
        for t, m in enumerate(maps):
            hi, lo = split(m)
            cm_w[i, WIN * t : WIN * (t + 1), 0:TILE] = hi
            cm_w[i, WIN * t : WIN * (t + 1), TILE : 2 * TILE] = lo

    loads["cols"].wait()
    loads["rim_cols"].wait()
    col_maps_of(0, 0, WIN)
    col_maps_of(
        1,
        jnp.where(n == 0, MARGIN, 0),
        jnp.where(n == NN - 1, MARGIN + TILE, WIN),
    )

    for c in plane:
        c.wait_recv()
    for side, dst in ((0, at), (1, ab)):
        rim_copy(dst, dst, side, 0, 1).wait_recv()
    blocks = [at] + [ar.at[k] for k in range(NQ)] + [ab]
    plane_rows = jnp.concatenate(
        [jnp.concatenate([b[0], b[1]], axis=1) for b in blocks], axis=0
    )
    a_h, a_l = split(
        jnp.concatenate([plane_rows[16 * k + 7 : 16 * k + 31] for k in range(NQ)], axis=0)
    )
    for c in sides:
        c.wait_recv()

    @pl.loop(0, COLS // 128)
    def _(j):
        at_j = pl.ds(pl.multiple_of(128 * j, 128), 128)
        b_h[:, at_j], b_l[:, at_j] = split(bx[:, at_j])

    loads["top"].wait()

    top_u[:, 0:32] = rm("top", 32)
    top_u[:, 32:64] = rm("top", 32)

    for c in outer:
        c.wait_recv()

    @pl.loop(0, 5)
    def _(j):
        start = pl.multiple_of(128 * jnp.minimum(2 * j, SPAN // 128 - 2), 128)
        here = pltpu.roll(q[:, pl.ds(start, 384)], 384 - MARGIN, 1)[:, 0:256]
        hi, lo = split(here)
        res = mm(mr[...], jnp.concatenate([hi, hi, lo], axis=0))
        at_j = pl.ds(start, 256)
        y_hl[0, :, at_j], y_hl[1, :, at_j] = split(res)

    @pl.loop(0, TILES)
    def _(j):
        at_rim = ((j == 0) & (n == 0)) | ((j == TILES - 1) & (n == NN - 1))
        at_j = pl.ds(pl.multiple_of(TILE * j, TILE), WIN)
        windows = [
            jnp.concatenate([y_hl[p, t * ROWS : (t + 1) * ROWS, at_j] for t in range(3)], axis=1)
            for p in range(2)
        ]
        both = mm(jnp.concatenate(windows, axis=0), cm_w[jnp.where(at_rim, 1, 0)])
        acc[:, pl.ds(pl.multiple_of(TILE * j, TILE), TILE)] = both[0:ROWS, 0:TILE] + (
            both[0:ROWS, TILE:] + both[ROWS:, 0:TILE]
        )

    results = [
        pltpu.make_async_copy(acc, near_out, out_s.at[0]),
        pltpu.make_async_copy(top_u, row_out, out_s.at[1]),
    ]
    for c in results:
        c.start()

    for c in column:
        c.wait_recv()
    g_h, g_l = split(g[...].reshape(256, 128))
    ps[...] = mm_both(a_h, a_l, g_h, g_l).reshape(NQ, 24, 128)

    partial_sums = []
    for i, (k, dx) in enumerate(hops):
        partial_sums.append(
            send(ps.at[rem(qi + k, NQ)], pa.at[xl, k], pa_s.at[i], pa_r.at[i], in_row(k, dx))
        )
    pa[xl, 0] = ps[qi]

    for c in partial_sums:
        c.wait_recv()
    for b in range(2):
        total = (pa[b, 0] + pa[b, 1]) + (pa[b, 2] + pa[b, 3])
        xb[y, :, 128 * b : 128 * (b + 1)] = total
    lines = [
        send(xb.at[y], xb.at[y], xb_s.at[k - 1], xb_r.at[k - 1], in_y(k)) for k in range(1, NY)
    ]

    for c in lines:
        c.wait_recv()
    lines_in = jnp.concatenate([xb[i] for i in range(NY)], axis=1)
    x_h, x_l = split(jnp.concatenate([lines_in, jnp.zeros((8, COLS), F32)], axis=0))
    with_hi = mm_nt(jnp.concatenate([x_h, x_l], axis=0), b_h[...])
    e_h, e_l = split(with_hi[0:32] + (with_hi[32:64] + mm_nt(x_h, b_l[...])))
    f_h, f_l = split(mm_left(e_h, e_l, ctop[...]))
    top_f[0:32, :] = f_h
    top_f[32:64, :] = f_l
    results.append(pltpu.make_async_copy(top_f, top_out, out_s.at[2]))
    results[-1].start()

    for c in rims + strips + plane + sides + outer + column + partial_sums + lines:
        c.wait_send()

    @pl.when(qi == NQ - 1)
    def _():
        for p in range(NQ):
            rim_down(p).wait_send()

    @pl.when(qi == 0)
    def _():
        for p in range(NQ):
            rim_up(p).wait_send()

    for c in results:
        c.wait()


def shards(maps, heat_power, level_taps, top_rows, top_cols):
    far_memory = pl.BlockSpec(memory_space=pltpu.HBM)
    sems = [10, 8, 8, 4, 4, 3, 3, 4, 2, 2, 2, 15, 15, 7, 7, 3, 3, 3]
    words = lambda *shape: pltpu.VMEM(shape, F32)
    halves = lambda *shape: pltpu.VMEM(shape, BF16)
    near, top, row = pl.pallas_call(
        kernel,
        out_shape=[
            jax.ShapeDtypeStruct((ROWS, COLS), F32),
            jax.ShapeDtypeStruct((64, COLS), BF16),
            jax.ShapeDtypeStruct((ROWS, 64), BF16),
        ],
        in_specs=[far_memory] * (4 + len(maps)),
        out_specs=[far_memory] * 3,
        scratch_shapes=[
            pltpu.SMEM((3, TAPS), F32),
            words(DEEP, WIDE),
            words(16, COLS),
            words(NQ, 2, 16, 128),
            words(NQ, 2, 16, 128),
            words(2, 8, 128),
            words(2, 8, 128),
            words(144, COLS),
            halves(*maps[0].shape[1:]),
            halves(2, *maps[1].shape[1:]),
            halves(*maps[2].shape[1:]),
            halves(*maps[3].shape[1:]),
            halves(*maps[4].shape),
            halves(3 * ROWS, 3 * DEEP),
            halves(2, 3 * ROWS, SPAN),
            halves(144, COLS),
            halves(144, COLS),
            halves(2, 3 * WIN, 2 * TILE),
            words(32, 384),
            words(8, 8, 128),
            words(2, 16, 128),
            words(NZ, 16, 128),
            words(NQ, 24, 128),
            words(2, NQ, 24, 128),
            words(NY, 24, 256),
            words(ROWS, COLS),
            halves(64, COLS),
            halves(ROWS, 64),
        ]
        + [pltpu.SemaphoreType.DMA((k,)) for k in sems],
        compiler_params=pltpu.CompilerParams(
            collective_id=0, has_side_effects=True, vmem_limit_bytes=62 * 1024 * 1024
        ),
    )(heat_power, level_taps, top_rows, top_cols, *maps)
    return near + mm(row, top)


def solution(mesh):
    maps = constants()
    return jax.shard_map(
        functools.partial(shards, maps),
        mesh=mesh,
        in_specs=(P("wide", "narrow"), P(), P("wide", None), P("narrow", None)),
        out_specs=P("wide", "narrow"),
        check_vma=False,
    )
```

```python
import functools

import jax
import jax.numpy as jnp
import ml_dtypes
import numpy as np
from jax import lax
from jax.experimental import pallas as pl
from jax.experimental.pallas import tpu as pltpu
from jax.sharding import PartitionSpec as P

F32 = jnp.float32
BF16 = jnp.bfloat16
MESH = pl.DeviceIdType.MESH
TAPS = 17
NZ, NQ, NN, NY = 16, 4, 8, 4
NW = NZ * NQ
ROWS, COLS = 128, 1024
HALO = 40
EXT = ROWS + 2 * HALO
DEEP = 256
SIDE = 128
WIDE = COLS + 2 * SIDE
TILE = 128
MARGIN = 64
WIN = TILE + 2 * MARGIN
SPAN = COLS + 2 * MARGIN
TILES = COLS // TILE


def restriction(out_n, out_off, in_n, in_off, first, out_end, in_end):
    out_at = np.arange(out_n)[:, None] + out_off
    in_at = np.arange(in_n)[None, :] + in_off
    d = in_at - 2 * out_at
    m = np.where((d == 0) | (d == 1), 0.375, 0.0) + np.where((d == -1) | (d == 2), 0.125, 0.0)
    if first:
        m = np.where((out_at >= 0) & (in_at >= 0), m, 0.0)
    if out_end is not None:
        m = np.where((out_at < out_end) & (in_at < in_end), m, 0.0)
    return m


def prolongation(out_n, out_off, in_n, in_off, first, in_end):
    out_at = np.arange(out_n)[:, None] + out_off
    in_at = np.arange(in_n)[None, :] + in_off
    d = out_at - 2 * in_at
    m = np.where((d == 0) | (d == 1), 0.75, 0.0) + np.where((d == -1) | (d == 2), 0.25, 0.0)
    if first:
        m = np.where(in_at >= 0, m, 0.0)
    if in_end is not None:
        m = np.where(in_at < in_end, m, 0.0)
    return m


def level_maps(block, off, size, variant):
    first, last = variant == 0, variant == 2
    end = [block >> t if last else None for t in range(4)]
    r1 = restriction(size // 2, -off // 2, size, -off, first, end[1], end[0])
    r2 = restriction(size // 4, -off // 4, size // 2, -off // 2, first, end[2], end[1])
    p1 = prolongation(block, 0, size // 2, -off // 2, first, end[1])
    p2 = prolongation(size // 2, -off // 2, size // 4, -off // 4, first, end[2])
    return r1, r2, p1, p2


def top_prolong(block, in_n, in_off, variant):
    first, last = variant == 0, variant == 2
    end = [block >> t if last else None for t in range(4)]
    p3 = prolongation(block // 4 + 4, -2, in_n, in_off, first, end[3])
    p2 = prolongation(block // 2 + 4, -2, block // 4 + 4, -2, first, end[2])
    p1 = prolongation(block, 0, block // 2 + 4, -2, first, end[1])
    return p1 @ p2 @ p3


def own_to_top(block, variant):
    first, last = variant == 0, variant == 2
    end = [block >> t if last else None for t in range(4)]
    r1 = restriction(block // 2 + 16, -8, block, 0, first, end[1], end[0])
    r2 = restriction(block // 4 + 16, -8, block // 2 + 16, -8, first, end[2], end[1])
    r3 = restriction(block // 8 + 16, -8, block // 4 + 16, -8, first, end[3], end[2])
    return r3 @ r2 @ r1


def padded(m, rows, cols):
    out = np.zeros((rows, cols))
    out[: m.shape[0], : m.shape[1]] = m
    return out


ROW_AT = dict(r3=(0, 32), r1=(32, 128), r21=(160, 64), p1=(224, 128), p12=(352, 128), top=(480, 128))
COL_AT = dict(r1=(0, 256), r21=(256, 256), p1=(512, 128), p12=(640, 64))


def constants():
    row_maps, col_maps, col_top, col_res = [], [], [], []
    for v in range(3):
        r1, r2, p1, p2 = level_maps(ROWS, HALO, EXT, v)
        row_maps.append(
            np.concatenate(
                [
                    padded(own_to_top(ROWS, v), 32, 256),
                    padded(r1, 128, 256),
                    padded(r2 @ r1, 64, 256),
                    padded(p1, 128, 256),
                    padded(p1 @ p2, 128, 256),
                    padded(top_prolong(ROWS, 24, -1, v), 128, 256),
                ]
            )
        )
        r1, r2, p1, p2 = level_maps(TILE, MARGIN, WIN, v)
        col_maps.append(
            np.concatenate([r1.T, padded((r2 @ r1).T, 256, 128), p1.T, (p1 @ p2).T])
        )
        res = own_to_top(COLS, v)
        col_res.append(np.concatenate([res[8:136], res[136:144], np.zeros((112, COLS)), res[0:8]]).T)
        col_top.append(top_prolong(COLS, 144, -8, v).T)
    at = np.arange(512)
    sort = np.zeros((512, 512))
    sort[at, 128 * (at // 16 % 4) + 16 * (at // 64) + at % 16] = 1.0
    as_bf16 = lambda ms: np.stack(ms).astype(ml_dtypes.bfloat16)
    return as_bf16(row_maps), as_bf16(col_maps), as_bf16(col_res), as_bf16(col_top), as_bf16(sort)


def split(x):
    hi = x.astype(BF16)
    return hi, (x - hi.astype(F32)).astype(BF16)


def mm(a, b):
    return jnp.dot(a, b, preferred_element_type=F32)


def mm_right(a, b_h, b_l):
    return mm(jnp.concatenate([a, a], axis=1), jnp.concatenate([b_h, b_l], axis=0))


def mm_left(a_h, a_l, b):
    res = mm(jnp.concatenate([a_h, a_l], axis=0), b)
    return res[0 : a_h.shape[0]] + res[a_h.shape[0] :]


def mm_both(a_h, a_l, b_h, b_l):
    m, n = a_h.shape[0], b_h.shape[1]
    res = mm(jnp.concatenate([a_h, a_l], axis=0), jnp.concatenate([b_h, b_l], axis=1))
    return res[0:m, 0:n] + (res[0:m, n:] + res[m:, 0:n])


def mm_nt(a, b):
    return lax.dot_general(a, b, (((1,), (1,)), ((), ())), preferred_element_type=F32)


def band(shape, in_dim, shift, taps, level):
    row = lax.broadcasted_iota(jnp.int32, (8, 256), 0)
    col = lax.broadcasted_iota(jnp.int32, (8, 256), 1)
    d = ((row - col if in_dim == 0 else col - row) + shift + 512) & 255
    first = jnp.zeros((8, 256), F32)
    for k in range(TAPS):
        first = jnp.where(d == k, taps[level, k], first)
    parts = [first] + [pltpu.roll(first, at, 1) for at in range(8, shape[0], 8)]
    return jnp.concatenate([p[:, 0 : shape[1]] for p in parts], axis=0)


def between(shape, dim, low, high):
    at = lax.broadcasted_iota(jnp.int32, shape, dim)
    return (at >= low) & (at < high)


def kernel(
    heat, taps_in, top_rows, top_cols, row_maps, col_maps, col_res, col_top, sort, near_out, top_out, row_out,
    taps, q, aw, to, ar, at, ab, bx, rmap, cmap, cres, ctop, perm,
    mr, y_hl, b_h, b_l, cm_w, es, nb, nb_mid, g, ps, pa, xb, acc, top_f, top_u,
    load_sem, rim_s, rim_r, halo_s, halo_r, aa_s, aa_r, ah_s, ah_r, bx_s, bx_r,
    z_s, z_r, pa_s, pa_r, xb_s, xb_r, out_s,
):
    w, n = lax.axis_index("wide"), lax.axis_index("narrow")
    rem = lax.rem
    z, qi = lax.div(w, NQ), rem(w, NQ)
    y, xl = lax.div(n, 2), rem(n, 2)
    row_at = z * NQ
    pair_at = n - xl

    def dev(dw, dn):
        return (rem(w + (dw + NW), NW) if dw else w, rem(n + (dn + NN), NN) if dn else n)

    def in_z(dz):
        return (rem(w + (dz + NZ) * NQ, NW), n)

    def in_row(k, dx):
        return (row_at + rem(qi + (k + NQ), NQ) if k else w, pair_at + 1 - xl if dx else n)

    def in_y(dy):
        return (w, rem(n + 2 * dy, NN))

    row_v = jnp.where(w == 0, 0, jnp.where(w == NW - 1, 2, 1))
    col_v = jnp.where(n == 0, 0, jnp.where(n == NN - 1, 2, 1))

    pairs = dict(
        heat=(heat, q.at[HALO : HALO + ROWS, SIDE : SIDE + COLS]),
        rows=(row_maps.at[row_v], rmap),
        res=(col_res.at[col_v], cres),
        top_rows=(top_rows, aw),
        sort=(sort, perm),
        top_cols=(top_cols, bx.at[8:136]),
        taps=(taps_in, taps),
        cols=(col_maps.at[1], cmap.at[0]),
        rim_cols=(col_maps.at[col_v], cmap.at[1]),
        top=(col_top.at[col_v], ctop),
    )
    loads = {
        name: pltpu.make_async_copy(src, dst, load_sem.at[i])
        for i, (name, (src, dst)) in enumerate(pairs.items())
    }
    for name in ("heat", "rows", "res"):
        loads[name].start()

    barrier = pltpu.get_barrier_semaphore()
    around = [(dw, dn) for dw in (-1, 0, 1) for dn in (-1, 0, 1) if (dw, dn) != (0, 0)]
    greet = [dev(dw, dn) for dw, dn in around]
    hops = [(k, dx) for k in range(NQ) for dx in range(2) if (k, dx) != (0, 0)]
    greet += [in_row(-k, dx) for k, dx in hops]
    greet += [in_y(dy) for dy in (1, 2, 3)]
    along = [8] + [d for dz in range(7, 0, -1) for d in (dz, -dz)]
    greet += [in_z(dz) for dz in along]
    count = len(greet)
    greet += [(rem(row_at + (NW - 1), NW), n), (rem(row_at + NQ, NW), n)]
    for target in greet:
        pl.semaphore_signal(barrier, inc=1, device_id=target, device_id_type=MESH)
    for name in ("top_rows", "sort", "top_cols", "taps", "cols", "rim_cols", "top"):
        loads[name].start()

    def send(src, dst, send_sem, recv_sem, target):
        c = pltpu.make_async_remote_copy(
            src_ref=src, dst_ref=dst, send_sem=send_sem, recv_sem=recv_sem,
            device_id=target, device_id_type=MESH,
        )
        c.start()
        return c

    def rm(name, cols):
        start, rows = ROW_AT[name]
        return rmap[start : start + rows, 0:cols]

    own_rows = slice(HALO, HALO + ROWS)

    def strip(src, dst, i, target):
        return send(q.at[src], q.at[dst], halo_s.at[i], halo_r.at[i], target)

    loads["heat"].wait()
    q[EXT:DEEP, :] = jnp.zeros((DEEP - EXT, WIDE), F32)

    loads["rows"].wait()
    loads["res"].wait()
    own_h, own_l = split(q[own_rows, SIDE : SIDE + COLS])
    r3 = rm("r3", ROWS)
    by_rows_h, by_rows_l = split(mm_right(r3, own_h, own_l))
    top = mm_left(by_rows_h, by_rows_l, cres[...])
    at_right = lax.broadcasted_iota(jnp.int32, (32, 128), 1) < 64
    es[:, 0:128] = jnp.where(at_right, 0.0, top[:, 128:256])
    es[:, 128:256] = top[:, 0:128]
    es[:, 256:384] = jnp.where(at_right, top[:, 128:256], 0.0)
    row_part = {-1: slice(0, 8), 0: slice(8, 24), 1: slice(24, 32)}
    col_part = {-1: slice(0, 128), 0: slice(128, 256), 1: slice(256, 384)}
    pl.semaphore_wait(barrier, jnp.where((qi == 0) | (qi == NQ - 1), count + NQ, count))
    rims = []
    for i, (dw, dn) in enumerate(around):
        dst = nb.at[i] if dw else nb_mid.at[i // 4]
        rims.append(
            send(es.at[row_part[dw], col_part[dn]], dst, rim_s.at[i], rim_r.at[i], dev(dw, dn))
        )

    strips = [
        strip((own_rows, slice(COLS, COLS + SIDE)), (own_rows, slice(0, SIDE)), 0, dev(0, 1)),
        strip((own_rows, slice(SIDE, 2 * SIDE)), (own_rows, slice(SIDE + COLS, WIDE)), 1, dev(0, -1)),
    ]

    loads["top_rows"].wait()
    loads["sort"].wait()
    halves = [split(aw[:, 512 * p : 512 * (p + 1)]) for p in range(2)]
    sorted_cols = mm(
        jnp.concatenate([halves[0][0], halves[1][0], halves[0][1], halves[1][1]], axis=0), perm[...]
    )
    sorted_cols = sorted_cols[0:32] + sorted_cols[32:64]
    for p in range(2):
        for k in range(NQ):
            to[k, p] = sorted_cols[16 * p : 16 * (p + 1), 128 * k : 128 * (k + 1)]
    plane = [
        send(to.at[rem(qi + k, NQ)], ar.at[qi], aa_s.at[k - 1], aa_r.at[k - 1], in_row(k, 0))
        for k in (1, 2, 3)
    ]
    ar[qi] = to[qi]

    def rim_copy(src, dst, side, p, dz):
        return pltpu.make_async_remote_copy(
            src_ref=src, dst_ref=dst, send_sem=ah_s.at[p], recv_sem=ah_r.at[side],
            device_id=(rem(row_at + ((dz + NZ) * NQ + p), NW), n), device_id_type=MESH,
        )

    def rim_down(p):
        return rim_copy(to.at[p, :, 8:16], at, 0, p, 1)

    def rim_up(p):
        return rim_copy(to.at[p, :, 0:8], ab, 1, p, -1)

    @pl.when(qi == NQ - 1)
    def _():
        for p in range(NQ):
            rim_down(p).start()

    @pl.when(qi == 0)
    def _():
        for p in range(NQ):
            rim_up(p).start()

    loads["top_cols"].wait()
    sides = [
        send(bx.at[128:136], bx.at[0:8], bx_s.at[0], bx_r.at[0], dev(0, 1)),
        send(bx.at[8:16], bx.at[136:144], bx_s.at[1], bx_r.at[1], dev(0, -1)),
    ]

    for c in strips:
        c.wait_recv()
    outer = [
        strip(slice(ROWS, ROWS + HALO), slice(0, HALO), 2, dev(1, 0)),
        strip(slice(HALO, 2 * HALO), slice(HALO + ROWS, EXT), 3, dev(-1, 0)),
    ]

    for c in rims:
        c.wait_recv()
    mid = nb_mid[0] + nb_mid[1]
    halves = [
        (es[8 + 8 * p : 16 + 8 * p, 128:256] + mid[8 * p : 8 * p + 8])
        + (nb[first] + (nb[first + 1] + nb[first + 2]))
        for p, first in ((0, 5), (1, 0))
    ]
    g[z] = jnp.concatenate(halves, axis=0)

    column = [
        send(g.at[z], g.at[z], z_s.at[i], z_r.at[i], in_z(dz)) for i, dz in enumerate(along)
    ]

    loads["taps"].wait()

    low, high = jnp.where(w == 0, HALO, 0), jnp.where(w == NW - 1, HALO + ROWS, EXT)
    t0 = jnp.where(
        between((ROWS, DEEP), 1, low, high), band((ROWS, DEEP), 1, 8 - HALO, taps, 0), 0.0
    )

    def row_level(level, size, res, pro):
        th, tl = split(band((size, size), 1, 8, taps, level))
        tr_h, tr_l = split(mm_left(th, tl, res))
        return mm_right(pro, tr_h, tr_l)

    row_maps_of = (
        t0,
        row_level(1, 128, rm("r1", DEEP), rm("p1", 128)),
        row_level(2, 64, rm("r21", DEEP), rm("p12", 64)),
    )
    for i, m in enumerate(row_maps_of):
        hi, lo = split(m)
        at_i = slice(i * ROWS, (i + 1) * ROWS)
        mr[at_i, 0:DEEP] = hi
        mr[at_i, DEEP : 2 * DEEP] = lo
        mr[at_i, 2 * DEEP : 3 * DEEP] = hi

    fine_band = band((WIN, TILE), 0, 8 - MARGIN, taps, 0)
    coarse_bands = [split(band((size, size), 0, 8, taps, t)) for t, size in ((1, 128), (2, 64))]

    def col_maps_of(i, low, high):
        def cm(name, cols):
            start, rows = COL_AT[name]
            return cmap[i, start : start + rows, 0:cols]

        maps = [jnp.where(between((WIN, TILE), 0, low, high), fine_band, 0.0)]
        for (th, tl), res, pro in (
            (coarse_bands[0], cm("r1", 128), cm("p1", 128)),
            (coarse_bands[1], cm("r21", 64), cm("p12", 128)),
        ):
            tp_h, tp_l = split(mm_left(th, tl, pro))
            maps.append(mm_right(res, tp_h, tp_l))
        for t, m in enumerate(maps):
            hi, lo = split(m)
            cm_w[i, WIN * t : WIN * (t + 1), 0:TILE] = hi
            cm_w[i, WIN * t : WIN * (t + 1), TILE : 2 * TILE] = lo

    loads["cols"].wait()
    loads["rim_cols"].wait()
    col_maps_of(0, 0, WIN)
    col_maps_of(
        1,
        jnp.where(n == 0, MARGIN, 0),
        jnp.where(n == NN - 1, MARGIN + TILE, WIN),
    )

    for c in plane:
        c.wait_recv()
    for side, dst in ((0, at), (1, ab)):
        rim_copy(dst, dst, side, 0, 1).wait_recv()
    blocks = [at] + [ar.at[k] for k in range(NQ)] + [ab]
    plane_rows = jnp.concatenate(
        [jnp.concatenate([b[0], b[1]], axis=1) for b in blocks], axis=0
    )
    a_h, a_l = split(
        jnp.concatenate([plane_rows[16 * k + 7 : 16 * k + 31] for k in range(NQ)], axis=0)
    )
    for c in sides:
        c.wait_recv()

    @pl.loop(0, COLS // 128)
    def _(j):
        at_j = pl.ds(pl.multiple_of(128 * j, 128), 128)
        b_h[:, at_j], b_l[:, at_j] = split(bx[:, at_j])

    loads["top"].wait()

    for c in column:
        c.wait_recv()
    g_h, g_l = split(g[...].reshape(256, 128))
    ps[...] = mm_both(a_h, a_l, g_h, g_l).reshape(NQ, 24, 128)

    partial_sums = []
    for i, (k, dx) in enumerate(hops):
        partial_sums.append(
            send(ps.at[rem(qi + k, NQ)], pa.at[xl, k], pa_s.at[i], pa_r.at[i], in_row(k, dx))
        )
    pa[xl, 0] = ps[qi]

    top_u[:, 0:32] = rm("top", 32)
    top_u[:, 32:64] = rm("top", 32)

    for c in outer:
        c.wait_recv()

    @pl.loop(0, 5)
    def _(j):
        start = pl.multiple_of(128 * jnp.minimum(2 * j, SPAN // 128 - 2), 128)
        here = pltpu.roll(q[:, pl.ds(start, 384)], 384 - MARGIN, 1)[:, 0:256]
        hi, lo = split(here)
        res = mm(mr[...], jnp.concatenate([hi, hi, lo], axis=0))
        at_j = pl.ds(start, 256)
        y_hl[0, :, at_j], y_hl[1, :, at_j] = split(res)

    for c in partial_sums:
        c.wait_recv()
    for b in range(2):
        total = (pa[b, 0] + pa[b, 1]) + (pa[b, 2] + pa[b, 3])
        xb[y, :, 128 * b : 128 * (b + 1)] = total
    lines = [
        send(xb.at[y], xb.at[y], xb_s.at[k - 1], xb_r.at[k - 1], in_y(k)) for k in range(1, NY)
    ]

    @pl.loop(0, TILES)
    def _(j):
        at_rim = ((j == 0) & (n == 0)) | ((j == TILES - 1) & (n == NN - 1))
        at_j = pl.ds(pl.multiple_of(TILE * j, TILE), WIN)
        windows = [
            jnp.concatenate([y_hl[p, t * ROWS : (t + 1) * ROWS, at_j] for t in range(3)], axis=1)
            for p in range(2)
        ]
        both = mm(jnp.concatenate(windows, axis=0), cm_w[jnp.where(at_rim, 1, 0)])
        acc[:, pl.ds(pl.multiple_of(TILE * j, TILE), TILE)] = both[0:ROWS, 0:TILE] + (
            both[0:ROWS, TILE:] + both[ROWS:, 0:TILE]
        )

    results = [
        pltpu.make_async_copy(acc, near_out, out_s.at[0]),
        pltpu.make_async_copy(top_u, row_out, out_s.at[1]),
    ]
    for c in results:
        c.start()

    for c in lines:
        c.wait_recv()
    lines_in = jnp.concatenate([xb[i] for i in range(NY)], axis=1)
    x_h, x_l = split(jnp.concatenate([lines_in, jnp.zeros((8, COLS), F32)], axis=0))
    with_hi = mm_nt(jnp.concatenate([x_h, x_l], axis=0), b_h[...])
    e_h, e_l = split(with_hi[0:32] + (with_hi[32:64] + mm_nt(x_h, b_l[...])))
    f_h, f_l = split(mm_left(e_h, e_l, ctop[...]))
    top_f[0:32, :] = f_h
    top_f[32:64, :] = f_l
    results.append(pltpu.make_async_copy(top_f, top_out, out_s.at[2]))
    results[-1].start()

    for c in rims + strips + plane + sides + outer + column + partial_sums + lines:
        c.wait_send()

    @pl.when(qi == NQ - 1)
    def _():
        for p in range(NQ):
            rim_down(p).wait_send()

    @pl.when(qi == 0)
    def _():
        for p in range(NQ):
            rim_up(p).wait_send()

    for c in results:
        c.wait()


def shards(maps, heat_power, level_taps, top_rows, top_cols):
    far_memory = pl.BlockSpec(memory_space=pltpu.HBM)
    sems = [10, 8, 8, 4, 4, 3, 3, 4, 2, 2, 2, 15, 15, 7, 7, 3, 3, 3]
    words = lambda *shape: pltpu.VMEM(shape, F32)
    halves = lambda *shape: pltpu.VMEM(shape, BF16)
    near, top, row = pl.pallas_call(
        kernel,
        out_shape=[
            jax.ShapeDtypeStruct((ROWS, COLS), F32),
            jax.ShapeDtypeStruct((64, COLS), BF16),
            jax.ShapeDtypeStruct((ROWS, 64), BF16),
        ],
        in_specs=[far_memory] * (4 + len(maps)),
        out_specs=[far_memory] * 3,
        scratch_shapes=[
            pltpu.SMEM((3, TAPS), F32),
            words(DEEP, WIDE),
            words(16, COLS),
            words(NQ, 2, 16, 128),
            words(NQ, 2, 16, 128),
            words(2, 8, 128),
            words(2, 8, 128),
            words(144, COLS),
            halves(*maps[0].shape[1:]),
            halves(2, *maps[1].shape[1:]),
            halves(*maps[2].shape[1:]),
            halves(*maps[3].shape[1:]),
            halves(*maps[4].shape),
            halves(3 * ROWS, 3 * DEEP),
            halves(2, 3 * ROWS, SPAN),
            halves(144, COLS),
            halves(144, COLS),
            halves(2, 3 * WIN, 2 * TILE),
            words(32, 384),
            words(8, 8, 128),
            words(2, 16, 128),
            words(NZ, 16, 128),
            words(NQ, 24, 128),
            words(2, NQ, 24, 128),
            words(NY, 24, 256),
            words(ROWS, COLS),
            halves(64, COLS),
            halves(ROWS, 64),
        ]
        + [pltpu.SemaphoreType.DMA((k,)) for k in sems],
        compiler_params=pltpu.CompilerParams(
            collective_id=0, has_side_effects=True, vmem_limit_bytes=62 * 1024 * 1024
        ),
    )(heat_power, level_taps, top_rows, top_cols, *maps)
    return near + mm(row, top)


def solution(mesh):
    maps = constants()
    return jax.shard_map(
        functools.partial(shards, maps),
        mesh=mesh,
        in_specs=(P("wide", "narrow"), P(), P("wide", None), P("narrow", None)),
        out_specs=P("wide", "narrow"),
        check_vma=False,
    )
```

```python
import functools

import jax
import jax.numpy as jnp
import ml_dtypes
import numpy as np
from jax import lax
from jax.experimental import pallas as pl
from jax.experimental.pallas import tpu as pltpu
from jax.sharding import PartitionSpec as P

F32 = jnp.float32
BF16 = jnp.bfloat16
MESH = pl.DeviceIdType.MESH
TAPS = 17
NZ, NQ, NN, NY = 16, 4, 8, 4
NW = NZ * NQ
ROWS, COLS = 128, 1024
HALO = 40
EXT = ROWS + 2 * HALO
DEEP = 256
SIDE = 128
WIDE = COLS + 2 * SIDE
TILE = 128
MARGIN = 64
WIN = TILE + 2 * MARGIN
SPAN = COLS + 2 * MARGIN
TILES = COLS // TILE


def restriction(out_n, out_off, in_n, in_off, first, out_end, in_end):
    out_at = np.arange(out_n)[:, None] + out_off
    in_at = np.arange(in_n)[None, :] + in_off
    d = in_at - 2 * out_at
    m = np.where((d == 0) | (d == 1), 0.375, 0.0) + np.where((d == -1) | (d == 2), 0.125, 0.0)
    if first:
        m = np.where((out_at >= 0) & (in_at >= 0), m, 0.0)
    if out_end is not None:
        m = np.where((out_at < out_end) & (in_at < in_end), m, 0.0)
    return m


def prolongation(out_n, out_off, in_n, in_off, first, in_end):
    out_at = np.arange(out_n)[:, None] + out_off
    in_at = np.arange(in_n)[None, :] + in_off
    d = out_at - 2 * in_at
    m = np.where((d == 0) | (d == 1), 0.75, 0.0) + np.where((d == -1) | (d == 2), 0.25, 0.0)
    if first:
        m = np.where(in_at >= 0, m, 0.0)
    if in_end is not None:
        m = np.where(in_at < in_end, m, 0.0)
    return m


def level_maps(block, off, size, variant):
    first, last = variant == 0, variant == 2
    end = [block >> t if last else None for t in range(4)]
    r1 = restriction(size // 2, -off // 2, size, -off, first, end[1], end[0])
    r2 = restriction(size // 4, -off // 4, size // 2, -off // 2, first, end[2], end[1])
    p1 = prolongation(block, 0, size // 2, -off // 2, first, end[1])
    p2 = prolongation(size // 2, -off // 2, size // 4, -off // 4, first, end[2])
    return r1, r2, p1, p2


def top_prolong(block, in_n, in_off, variant):
    first, last = variant == 0, variant == 2
    end = [block >> t if last else None for t in range(4)]
    p3 = prolongation(block // 4 + 4, -2, in_n, in_off, first, end[3])
    p2 = prolongation(block // 2 + 4, -2, block // 4 + 4, -2, first, end[2])
    p1 = prolongation(block, 0, block // 2 + 4, -2, first, end[1])
    return p1 @ p2 @ p3


def own_to_top(block, variant):
    first, last = variant == 0, variant == 2
    end = [block >> t if last else None for t in range(4)]
    r1 = restriction(block // 2 + 16, -8, block, 0, first, end[1], end[0])
    r2 = restriction(block // 4 + 16, -8, block // 2 + 16, -8, first, end[2], end[1])
    r3 = restriction(block // 8 + 16, -8, block // 4 + 16, -8, first, end[3], end[2])
    return r3 @ r2 @ r1


def padded(m, rows, cols):
    out = np.zeros((rows, cols))
    out[: m.shape[0], : m.shape[1]] = m
    return out


ROW_AT = dict(r3=(0, 32), r1=(32, 128), r21=(160, 64), p1=(224, 128), p12=(352, 128), top=(480, 128))
COL_AT = dict(r1=(0, 256), r21=(256, 256), p1=(512, 128), p12=(640, 64))


def constants():
    row_maps, col_maps, col_top, col_res = [], [], [], []
    for v in range(3):
        r1, r2, p1, p2 = level_maps(ROWS, HALO, EXT, v)
        row_maps.append(
            np.concatenate(
                [
                    padded(own_to_top(ROWS, v), 32, 256),
                    padded(r1, 128, 256),
                    padded(r2 @ r1, 64, 256),
                    padded(np.concatenate([p1[:, 12:92], (p1 @ p2)[:, 2:50]], 1), 128, 256),
                    padded(p1 @ p2, 128, 256),
                    padded(top_prolong(ROWS, 24, -1, v), 128, 256),
                ]
            )
        )
        r1, r2, p1, p2 = level_maps(TILE, MARGIN, WIN, v)
        col_maps.append(
            np.concatenate([r1.T, padded((r2 @ r1).T, 256, 128), p1.T, (p1 @ p2).T])
        )
        res = own_to_top(COLS, v)
        col_res.append(np.concatenate([res[8:136], res[136:144], np.zeros((112, COLS)), res[0:8]]).T)
        col_top.append(top_prolong(COLS, 144, -8, v).T)
    at = np.arange(512)
    sort = np.zeros((512, 512))
    sort[at, 128 * (at // 16 % 4) + 16 * (at // 64) + at % 16] = 1.0
    as_bf16 = lambda ms: np.stack(ms).astype(ml_dtypes.bfloat16)
    return as_bf16(row_maps), as_bf16(col_maps), as_bf16(col_res), as_bf16(col_top), as_bf16(sort)


def split(x):
    hi = x.astype(BF16)
    return hi, (x - hi.astype(F32)).astype(BF16)


def mm(a, b):
    return jnp.dot(a, b, preferred_element_type=F32)


def mm_right(a, b_h, b_l):
    return mm(jnp.concatenate([a, a], axis=1), jnp.concatenate([b_h, b_l], axis=0))


def mm_left(a_h, a_l, b):
    res = mm(jnp.concatenate([a_h, a_l], axis=0), b)
    return res[0 : a_h.shape[0]] + res[a_h.shape[0] :]


def mm_both(a_h, a_l, b_h, b_l):
    m, n = a_h.shape[0], b_h.shape[1]
    res = mm(jnp.concatenate([a_h, a_l], axis=0), jnp.concatenate([b_h, b_l], axis=1))
    return res[0:m, 0:n] + (res[0:m, n:] + res[m:, 0:n])


def mm_nt(a, b):
    return lax.dot_general(a, b, (((1,), (1,)), ((), ())), preferred_element_type=F32)


def band(shape, in_dim, shift, taps, level):
    row = lax.broadcasted_iota(jnp.int32, (8, 256), 0)
    col = lax.broadcasted_iota(jnp.int32, (8, 256), 1)
    d = ((row - col if in_dim == 0 else col - row) + shift + 512) & 255
    first = jnp.zeros((8, 256), F32)
    for k in range(TAPS):
        first = jnp.where(d == k, taps[level, k], first)
    parts = [first] + [pltpu.roll(first, at, 1) for at in range(8, shape[0], 8)]
    return jnp.concatenate([p[:, 0 : shape[1]] for p in parts], axis=0)


def between(shape, dim, low, high):
    at = lax.broadcasted_iota(jnp.int32, shape, dim)
    return (at >= low) & (at < high)


def kernel(
    heat, taps_in, top_rows, top_cols, row_maps, col_maps, col_res, col_top, sort, near_out, top_out, row_out,
    taps, q, aw, to, ar, at, ab, bx, rmap, cmap, cres, ctop, perm,
    mr, y_hl, b_h, b_l, cm_w, es, nb, nb_mid, g, ps, pa, xb, acc, top_f, top_u,
    load_sem, rim_s, rim_r, halo_s, halo_r, aa_s, aa_r, ah_s, ah_r, bx_s, bx_r,
    z_s, z_r, pa_s, pa_r, xb_s, xb_r, out_s,
):
    w, n = lax.axis_index("wide"), lax.axis_index("narrow")
    rem = lax.rem
    z, qi = lax.div(w, NQ), rem(w, NQ)
    y, xl = lax.div(n, 2), rem(n, 2)
    row_at = z * NQ
    pair_at = n - xl

    def dev(dw, dn):
        return (rem(w + (dw + NW), NW) if dw else w, rem(n + (dn + NN), NN) if dn else n)

    def in_z(dz):
        return (rem(w + (dz + NZ) * NQ, NW), n)

    def in_row(k, dx):
        return (row_at + rem(qi + (k + NQ), NQ) if k else w, pair_at + 1 - xl if dx else n)

    def in_y(dy):
        return (w, rem(n + 2 * dy, NN))

    row_v = jnp.where(w == 0, 0, jnp.where(w == NW - 1, 2, 1))
    col_v = jnp.where(n == 0, 0, jnp.where(n == NN - 1, 2, 1))

    pairs = dict(
        heat=(heat, q.at[HALO : HALO + ROWS, SIDE : SIDE + COLS]),
        rows=(row_maps.at[row_v], rmap),
        res=(col_res.at[col_v], cres),
        top_rows=(top_rows, aw),
        sort=(sort, perm),
        top_cols=(top_cols, bx.at[8:136]),
        taps=(taps_in, taps),
        cols=(col_maps.at[1], cmap.at[0]),
        rim_cols=(col_maps.at[col_v], cmap.at[1]),
        top=(col_top.at[col_v], ctop),
    )
    loads = {
        name: pltpu.make_async_copy(src, dst, load_sem.at[i])
        for i, (name, (src, dst)) in enumerate(pairs.items())
    }
    for name in ("heat", "rows", "res"):
        loads[name].start()

    barrier = pltpu.get_barrier_semaphore()
    around = [(dw, dn) for dw in (-1, 0, 1) for dn in (-1, 0, 1) if (dw, dn) != (0, 0)]
    greet = [dev(dw, dn) for dw, dn in around]
    hops = [(k, dx) for k in range(NQ) for dx in range(2) if (k, dx) != (0, 0)]
    greet += [in_row(-k, dx) for k, dx in hops]
    greet += [in_y(dy) for dy in (1, 2, 3)]
    along = [8] + [d for dz in range(7, 0, -1) for d in (dz, -dz)]
    greet += [in_z(dz) for dz in along]
    count = len(greet)
    greet += [(rem(row_at + (NW - 1), NW), n), (rem(row_at + NQ, NW), n)]
    for target in greet:
        pl.semaphore_signal(barrier, inc=1, device_id=target, device_id_type=MESH)
    for name in ("top_rows", "sort", "top_cols", "taps", "cols", "rim_cols", "top"):
        loads[name].start()

    def send(src, dst, send_sem, recv_sem, target):
        c = pltpu.make_async_remote_copy(
            src_ref=src, dst_ref=dst, send_sem=send_sem, recv_sem=recv_sem,
            device_id=target, device_id_type=MESH,
        )
        c.start()
        return c

    def rm(name, cols):
        start, rows = ROW_AT[name]
        return rmap[start : start + rows, 0:cols]

    own_rows = slice(HALO, HALO + ROWS)

    def strip(src, dst, i, target):
        return send(q.at[src], q.at[dst], halo_s.at[i], halo_r.at[i], target)

    loads["heat"].wait()
    q[EXT:DEEP, :] = jnp.zeros((DEEP - EXT, WIDE), F32)

    loads["rows"].wait()
    loads["res"].wait()
    own_h, own_l = split(q[own_rows, SIDE : SIDE + COLS])
    r3 = rm("r3", ROWS)
    by_rows_h, by_rows_l = split(mm_right(r3, own_h, own_l))
    top = mm_left(by_rows_h, by_rows_l, cres[...])
    at_right = lax.broadcasted_iota(jnp.int32, (32, 128), 1) < 64
    es[:, 0:128] = jnp.where(at_right, 0.0, top[:, 128:256])
    es[:, 128:256] = top[:, 0:128]
    es[:, 256:384] = jnp.where(at_right, top[:, 128:256], 0.0)
    row_part = {-1: slice(0, 8), 0: slice(8, 24), 1: slice(24, 32)}
    col_part = {-1: slice(0, 128), 0: slice(128, 256), 1: slice(256, 384)}
    pl.semaphore_wait(barrier, jnp.where((qi == 0) | (qi == NQ - 1), count + NQ, count))
    rims = []
    for i, (dw, dn) in enumerate(around):
        dst = nb.at[i] if dw else nb_mid.at[i // 4]
        rims.append(
            send(es.at[row_part[dw], col_part[dn]], dst, rim_s.at[i], rim_r.at[i], dev(dw, dn))
        )

    strips = [
        strip((own_rows, slice(COLS, COLS + SIDE)), (own_rows, slice(0, SIDE)), 0, dev(0, 1)),
        strip((own_rows, slice(SIDE, 2 * SIDE)), (own_rows, slice(SIDE + COLS, WIDE)), 1, dev(0, -1)),
    ]

    loads["top_rows"].wait()
    loads["sort"].wait()
    halves = [split(aw[:, 512 * p : 512 * (p + 1)]) for p in range(2)]
    sorted_cols = mm(
        jnp.concatenate([halves[0][0], halves[1][0], halves[0][1], halves[1][1]], axis=0), perm[...]
    )
    sorted_cols = sorted_cols[0:32] + sorted_cols[32:64]
    for p in range(2):
        for k in range(NQ):
            to[k, p] = sorted_cols[16 * p : 16 * (p + 1), 128 * k : 128 * (k + 1)]
    plane = [
        send(to.at[rem(qi + k, NQ)], ar.at[qi], aa_s.at[k - 1], aa_r.at[k - 1], in_row(k, 0))
        for k in (1, 2, 3)
    ]
    ar[qi] = to[qi]

    def rim_copy(src, dst, side, p, dz):
        return pltpu.make_async_remote_copy(
            src_ref=src, dst_ref=dst, send_sem=ah_s.at[p], recv_sem=ah_r.at[side],
            device_id=(rem(row_at + ((dz + NZ) * NQ + p), NW), n), device_id_type=MESH,
        )

    def rim_down(p):
        return rim_copy(to.at[p, :, 8:16], at, 0, p, 1)

    def rim_up(p):
        return rim_copy(to.at[p, :, 0:8], ab, 1, p, -1)

    @pl.when(qi == NQ - 1)
    def _():
        for p in range(NQ):
            rim_down(p).start()

    @pl.when(qi == 0)
    def _():
        for p in range(NQ):
            rim_up(p).start()

    loads["top_cols"].wait()
    sides = [
        send(bx.at[128:136], bx.at[0:8], bx_s.at[0], bx_r.at[0], dev(0, 1)),
        send(bx.at[8:16], bx.at[136:144], bx_s.at[1], bx_r.at[1], dev(0, -1)),
    ]

    for c in strips:
        c.wait_recv()
    outer = [
        strip(slice(ROWS, ROWS + HALO), slice(0, HALO), 2, dev(1, 0)),
        strip(slice(HALO, 2 * HALO), slice(HALO + ROWS, EXT), 3, dev(-1, 0)),
    ]

    for c in rims:
        c.wait_recv()
    mid = nb_mid[0] + nb_mid[1]
    halves = [
        (es[8 + 8 * p : 16 + 8 * p, 128:256] + mid[8 * p : 8 * p + 8])
        + (nb[first] + (nb[first + 1] + nb[first + 2]))
        for p, first in ((0, 5), (1, 0))
    ]
    g[z] = jnp.concatenate(halves, axis=0)

    column = [
        send(g.at[z], g.at[z], z_s.at[i], z_r.at[i], in_z(dz)) for i, dz in enumerate(along)
    ]

    loads["taps"].wait()

    low, high = jnp.where(w == 0, HALO, 0), jnp.where(w == NW - 1, HALO + ROWS, EXT)
    t0 = jnp.where(
        between((ROWS, DEEP), 1, low, high), band((ROWS, DEEP), 1, 8 - HALO, taps, 0), 0.0
    )

    def row_level(level, shape, shift, res):
        th, tl = split(band(shape, 1, shift, taps, level))
        return mm_left(th, tl, res)

    row_maps_of = jnp.concatenate(
        [
            t0,
            row_level(1, (80, 128), -4, rm("r1", DEEP)),
            row_level(2, (48, 64), 6, rm("r21", DEEP)),
        ],
        axis=0,
    )
    hi, lo = split(row_maps_of)
    mr[:, 0:DEEP] = hi
    mr[:, DEEP : 2 * DEEP] = lo
    mr[:, 2 * DEEP : 3 * DEEP] = hi

    fine_band = band((WIN, TILE), 0, 8 - MARGIN, taps, 0)
    coarse_bands = [split(band((size, size), 0, 8, taps, t)) for t, size in ((1, 128), (2, 64))]

    def col_maps_of(i, low, high):
        def cm(name, cols):
            start, rows = COL_AT[name]
            return cmap[i, start : start + rows, 0:cols]

        maps = [jnp.where(between((WIN, TILE), 0, low, high), fine_band, 0.0)]
        for (th, tl), res, pro in (
            (coarse_bands[0], cm("r1", 128), cm("p1", 128)),
            (coarse_bands[1], cm("r21", 64), cm("p12", 128)),
        ):
            tp_h, tp_l = split(mm_left(th, tl, pro))
            maps.append(mm_right(res, tp_h, tp_l))
        for t, m in enumerate(maps):
            hi, lo = split(m)
            cm_w[i, WIN * t : WIN * (t + 1), 0:TILE] = hi
            cm_w[i, WIN * t : WIN * (t + 1), TILE : 2 * TILE] = lo

    loads["cols"].wait()
    loads["rim_cols"].wait()
    col_maps_of(0, 0, WIN)
    col_maps_of(
        1,
        jnp.where(n == 0, MARGIN, 0),
        jnp.where(n == NN - 1, MARGIN + TILE, WIN),
    )

    for c in plane:
        c.wait_recv()
    for side, dst in ((0, at), (1, ab)):
        rim_copy(dst, dst, side, 0, 1).wait_recv()
    blocks = [at] + [ar.at[k] for k in range(NQ)] + [ab]
    plane_rows = jnp.concatenate(
        [jnp.concatenate([b[0], b[1]], axis=1) for b in blocks], axis=0
    )
    a_h, a_l = split(
        jnp.concatenate([plane_rows[16 * k + 7 : 16 * k + 31] for k in range(NQ)], axis=0)
    )
    for c in sides:
        c.wait_recv()

    @pl.loop(0, COLS // 128)
    def _(j):
        at_j = pl.ds(pl.multiple_of(128 * j, 128), 128)
        b_h[:, at_j], b_l[:, at_j] = split(bx[:, at_j])

    loads["top"].wait()

    for c in column:
        c.wait_recv()
    g_h, g_l = split(g[...].reshape(256, 128))
    ps[...] = mm_both(a_h, a_l, g_h, g_l).reshape(NQ, 24, 128)

    partial_sums = []
    for i, (k, dx) in enumerate(hops):
        partial_sums.append(
            send(ps.at[rem(qi + k, NQ)], pa.at[xl, k], pa_s.at[i], pa_r.at[i], in_row(k, dx))
        )
    pa[xl, 0] = ps[qi]

    top_u[:, 0:32] = rm("top", 32)
    top_u[:, 32:64] = rm("top", 32)

    for c in outer:
        c.wait_recv()

    @pl.loop(0, 5)
    def _(j):
        start = pl.multiple_of(128 * jnp.minimum(2 * j, SPAN // 128 - 2), 128)
        here = pltpu.roll(q[:, pl.ds(start, 384)], 384 - MARGIN, 1)[:, 0:256]
        hi, lo = split(here)
        res = mm(mr[...], jnp.concatenate([hi, hi, lo], axis=0))
        at_j = pl.ds(start, 256)
        y_hl[0, :, at_j], y_hl[1, :, at_j] = split(res)

    for c in partial_sums:
        c.wait_recv()
    for b in range(2):
        total = (pa[b, 0] + pa[b, 1]) + (pa[b, 2] + pa[b, 3])
        xb[y, :, 128 * b : 128 * (b + 1)] = total
    lines = [
        send(xb.at[y], xb.at[y], xb_s.at[k - 1], xb_r.at[k - 1], in_y(k)) for k in range(1, NY)
    ]

    @pl.loop(0, TILES)
    def _(j):
        at_rim = ((j == 0) & (n == 0)) | ((j == TILES - 1) & (n == NN - 1))
        at_j = pl.ds(pl.multiple_of(TILE * j, TILE), WIN)
        which = jnp.where(at_rim, 1, 0)
        levels = []
        for t, (low, high) in enumerate(((0, 128), (128, 208), (208, 256))):
            m = high - low
            both = mm(
                jnp.concatenate([y_hl[0, low:high, at_j], y_hl[1, low:high, at_j]], axis=0),
                cm_w[which, WIN * t : WIN * (t + 1)],
            )
            levels.append(both[0:m, 0:TILE] + (both[0:m, TILE:] + both[m:, 0:TILE]))
        z_h, z_l = split(jnp.concatenate(levels[1:], axis=0))
        acc[:, pl.ds(pl.multiple_of(TILE * j, TILE), TILE)] = levels[0] + mm_right(
            rm("p1", 128), z_h, z_l
        )

    results = [
        pltpu.make_async_copy(acc, near_out, out_s.at[0]),
        pltpu.make_async_copy(top_u, row_out, out_s.at[1]),
    ]
    for c in results:
        c.start()

    for c in lines:
        c.wait_recv()
    lines_in = jnp.concatenate([xb[i] for i in range(NY)], axis=1)
    x_h, x_l = split(jnp.concatenate([lines_in, jnp.zeros((8, COLS), F32)], axis=0))
    with_hi = mm_nt(jnp.concatenate([x_h, x_l], axis=0), b_h[...])
    e_h, e_l = split(with_hi[0:32] + (with_hi[32:64] + mm_nt(x_h, b_l[...])))
    f_h, f_l = split(mm_left(e_h, e_l, ctop[...]))
    top_f[0:32, :] = f_h
    top_f[32:64, :] = f_l
    results.append(pltpu.make_async_copy(top_f, top_out, out_s.at[2]))
    results[-1].start()

    for c in rims + strips + plane + sides + outer + column + partial_sums + lines:
        c.wait_send()

    @pl.when(qi == NQ - 1)
    def _():
        for p in range(NQ):
            rim_down(p).wait_send()

    @pl.when(qi == 0)
    def _():
        for p in range(NQ):
            rim_up(p).wait_send()

    for c in results:
        c.wait()


def shards(maps, heat_power, level_taps, top_rows, top_cols):
    far_memory = pl.BlockSpec(memory_space=pltpu.HBM)
    sems = [10, 8, 8, 4, 4, 3, 3, 4, 2, 2, 2, 15, 15, 7, 7, 3, 3, 3]
    words = lambda *shape: pltpu.VMEM(shape, F32)
    halves = lambda *shape: pltpu.VMEM(shape, BF16)
    near, top, row = pl.pallas_call(
        kernel,
        out_shape=[
            jax.ShapeDtypeStruct((ROWS, COLS), F32),
            jax.ShapeDtypeStruct((64, COLS), BF16),
            jax.ShapeDtypeStruct((ROWS, 64), BF16),
        ],
        in_specs=[far_memory] * (4 + len(maps)),
        out_specs=[far_memory] * 3,
        scratch_shapes=[
            pltpu.SMEM((3, TAPS), F32),
            words(DEEP, WIDE),
            words(16, COLS),
            words(NQ, 2, 16, 128),
            words(NQ, 2, 16, 128),
            words(2, 8, 128),
            words(2, 8, 128),
            words(144, COLS),
            halves(*maps[0].shape[1:]),
            halves(2, *maps[1].shape[1:]),
            halves(*maps[2].shape[1:]),
            halves(*maps[3].shape[1:]),
            halves(*maps[4].shape),
            halves(2 * ROWS, 3 * DEEP),
            halves(2, 2 * ROWS, SPAN),
            halves(144, COLS),
            halves(144, COLS),
            halves(2, 3 * WIN, 2 * TILE),
            words(32, 384),
            words(8, 8, 128),
            words(2, 16, 128),
            words(NZ, 16, 128),
            words(NQ, 24, 128),
            words(2, NQ, 24, 128),
            words(NY, 24, 256),
            words(ROWS, COLS),
            halves(64, COLS),
            halves(ROWS, 64),
        ]
        + [pltpu.SemaphoreType.DMA((k,)) for k in sems],
        compiler_params=pltpu.CompilerParams(
            collective_id=0, has_side_effects=True, vmem_limit_bytes=62 * 1024 * 1024
        ),
    )(heat_power, level_taps, top_rows, top_cols, *maps)
    return near + mm(row, top)


def solution(mesh):
    maps = constants()
    return jax.shard_map(
        functools.partial(shards, maps),
        mesh=mesh,
        in_specs=(P("wide", "narrow"), P(), P("wide", None), P("narrow", None)),
        out_specs=P("wide", "narrow"),
        check_vma=False,
    )
```
